32 devices in a mesh: dp: 4 (over y, x), tensor: 8 (over z, core).
Axes of the slice: x: 2, y: 2, z: 4, core: 2. Of those that a mesh axis runs over, the one named last changes fastest.
Arguments:
- hidden: bfloat16 [2048, 53248], P('dp', 'tensor'), may hold values from -6 to 6
- cotangent: bfloat16 [2048, 16384], P('dp', 'tensor'), may hold values from -96 to 96
- prompt_group_index: int32 [2048], P('dp'), may hold values from 0 to 255
- answer_token_mask: int32 [2048], P('dp'), may hold values 0 or 1
- token_reward_order: int32 [2048], P('dp'), may hold values from 0 to 15
- source_lowdim_matrix: float32 [32, 53248], P(None, 'tensor'), may hold values from -0.02734375 to 0.02734375
- running_mean_source_matrix: float32 [32, 53248], P(None, 'tensor'), may hold values from -6 to 6
- running_variance_source_matrix: float32 [32, 53248], P(None, 'tensor'), may hold values from 0.01 to 1
- target_lowdim_matrix: float32 [32, 16384], P(None, 'tensor'), may hold values from -1 to 1
- running_mean_target_matrix: float32 [32, 16384], P(None, 'tensor'), may hold values from -0.6 to 0.6
- running_variance_target_matrix: float32 [32, 16384], P(None, 'tensor'), may hold values from 0.0001 to 0.01
- frozen_down_weight: bfloat16 [53248, 16384], P('tensor', 'dp'), may hold values from -0.02734375 to 0.02734375
- sampled_token_input: bfloat16 [512, 53248], P(None, 'tensor'), may hold values from -6 to 6
Outputs:
- rollout_out: bfloat16 [512, 16384], P(None, ('dp', 'tensor'))
- next_left_factor: float32 [32, 53248], P('dp', 'tensor')
- next_first_moment_left: float32 [32, 53248], P('dp', 'tensor')
- next_second_moment_left: float32 [32, 53248], P('dp', 'tensor')
- next_right_factor: float32 [32, 16384], P('dp', 'tensor')
- next_first_moment_right: float32 [32, 16384], P('dp', 'tensor')
- next_second_moment_right: float32 [32, 16384], P('dp', 'tensor')
The draws below stay inside these ranges and needn't reach their ends.
All inputs are finite; a program needn't handle non-finite values. No bound on the sum of `answer_token_mask` on one device may be relied on, other than what follows from the above.
Results may differ from the reference program's by a relative error of at most 0.0063.
Values may be sent and summed in bfloat16 or wider, within the bound.
No kernel may reach another device: no remote copies, remote signals or barrier semaphores. Data moves between devices by JAX's collectives and lax.ppermute only.
A program may use at most 192 MiB of HBM per device.

```python
import math
import jax
import jax.numpy as jnp
from jax import lax

EMBEDDING_SIZE = 16384
INNER_NEURONS = 53248
LATENT_DIMENSION = 32
ROLLOUT = 512
TOKENS = 2048
GROUPS = 256
N_TENSOR = 8


def with_ends(entries, stream_key, smallest, high):
    index_at = [jax.random.randint(jax.random.fold_in(stream_key, axis), (), 0, length) for axis, length in enumerate(entries.shape)]
    main_axis = entries.shape.index(max(entries.shape))
    next_to = index_at[:main_axis] + [(index_at[main_axis] + 1) % entries.shape[main_axis]] + index_at[main_axis + 1:]
    return entries.at[tuple(index_at)].set(smallest).at[tuple(next_to)].set(high)


def level_of(key, shape, split, low, largest):
    level, own = 1.0, jax.random.fold_in(key, 6)
    for axis_at, blocks in split:
        steps = jnp.exp(jax.random.uniform(jax.random.fold_in(own, axis_at), (blocks,), jnp.float32, low / len(split), largest / len(split)))
        level = level * jnp.repeat(steps, shape[axis_at] // blocks).reshape([-1 if axis == axis_at else 1 for axis in range(len(shape))])
    return level


def gaussian(own_key, extent, deviation, bound, shards=(), kind=jnp.bfloat16):
    entries = deviation * jax.random.normal(own_key, extent, jnp.float32)
    if shards:
        entries = entries * level_of(own_key, extent, shards, -0.22, 0.18)
    return jnp.clip(entries, -bound, bound).astype(kind)


def setup_inputs(seed: int = 0) -> dict:
    streams_of = jax.random.split(jax.random.key(seed), 14)
    return {
        "hidden": gaussian(streams_of[0], (TOKENS, INNER_NEURONS), 1.0, 6.0, ((0, 4), (1, 8))),
        "cotangent": gaussian(streams_of[1], (TOKENS, EMBEDDING_SIZE), 16.0, 96.0, ((0, 4), (1, 8))),
        "prompt_group_index": with_ends(jax.random.randint(streams_of[2], (TOKENS,), 0, GROUPS), jax.random.fold_in(streams_of[2], 1), 0, GROUPS - 1).astype(jnp.int32),
        "answer_token_mask": with_ends((jax.random.randint(streams_of[3], (TOKENS,), 0, 4) < 3).astype(jnp.int32), jax.random.fold_in(streams_of[3], 1), 0, 1),
        "token_reward_order": with_ends(jax.random.randint(streams_of[4], (TOKENS,), 0, 16), jax.random.fold_in(streams_of[4], 1), 0, 15).astype(jnp.int32),
        "source_lowdim_matrix": gaussian(streams_of[5], (LATENT_DIMENSION, INNER_NEURONS), INNER_NEURONS ** -0.5, 0.02734375, ((1, 8),), jnp.float32),
        "running_mean_source_matrix": gaussian(streams_of[6], (LATENT_DIMENSION, INNER_NEURONS), 1.0, 6.0, ((1, 8),), jnp.float32),
        "running_variance_source_matrix": jnp.clip(jnp.exp(math.log(1.0) - 4.6051702 * jax.random.uniform(streams_of[7], (LATENT_DIMENSION, INNER_NEURONS), jnp.float32) ** level_of(streams_of[7], (LATENT_DIMENSION, INNER_NEURONS), ((1, 8),), -0.2, 0.2)), 0.01, 1.0),
        "target_lowdim_matrix": gaussian(streams_of[8], (LATENT_DIMENSION, EMBEDDING_SIZE), LATENT_DIMENSION ** -0.5, 1.0, ((1, 8),), jnp.float32),
        "running_mean_target_matrix": gaussian(streams_of[9], (LATENT_DIMENSION, EMBEDDING_SIZE), 0.1, 0.6, ((1, 8),), jnp.float32),
        "running_variance_target_matrix": jnp.clip(jnp.exp(math.log(0.01) - 4.6051702 * jax.random.uniform(streams_of[10], (LATENT_DIMENSION, EMBEDDING_SIZE), jnp.float32) ** level_of(streams_of[10], (LATENT_DIMENSION, EMBEDDING_SIZE), ((1, 8),), -0.2, 0.2)), 0.0001, 0.01),
        "frozen_down_weight": gaussian(streams_of[11], (INNER_NEURONS, EMBEDDING_SIZE), INNER_NEURONS ** -0.5, 0.02734375, ((0, 8), (1, 4))),
        "sampled_token_input": gaussian(streams_of[12], (ROLLOUT, INNER_NEURONS), 1.0, 6.0, ((1, 8),)),
    }


adapter_scale = 2.0
bias_one = 1.0 - 0.9 ** 10
bias_two = 1.0 - 0.999 ** 10

def adaptive_moment_step(param, grad, first, second):
    first = 0.9 * first + 0.1 * grad
    second = 0.999 * second + 0.001 * grad * grad
    param = param - 0.004 * (first / bias_one) / (jnp.sqrt(second / bias_two) + 1e-08)
    return (param, first, second)

def reference(hidden, cotangent, prompt_group_index, answer_token_mask, token_reward_order, source_lowdim_matrix, running_mean_source_matrix, running_variance_source_matrix, target_lowdim_matrix, running_mean_target_matrix, running_variance_target_matrix, frozen_down_weight, sampled_token_input):
    left_factor_value = source_lowdim_matrix.astype(jnp.bfloat16)
    rank_projection = jnp.dot(hidden, left_factor_value.T, preferred_element_type=jnp.float32)
    mask_float = answer_token_mask.astype(jnp.float32)
    rank_float = token_reward_order.astype(jnp.float32)
    member = (prompt_group_index[:, None] == jnp.arange(GROUPS, dtype=jnp.int32)[None, :]).astype(jnp.float32)
    masked = member * mask_float[:, None]
    counts = lax.optimization_barrier(jnp.sum(masked, axis=0))
    sums = lax.optimization_barrier(jnp.sum(masked * rank_float[:, None], axis=0))
    squares = lax.optimization_barrier(jnp.sum(masked * (rank_float * rank_float)[:, None], axis=0))
    safe_counts = jnp.maximum(counts, 1.0)
    mean = sums / safe_counts
    spread = jnp.maximum(jnp.sqrt(jnp.maximum(squares / safe_counts - mean * mean, 0.0)), 1.0)
    total = jnp.maximum(jnp.sum(counts), 1.0)
    coefficient = -mask_float * (rank_float - mean[prompt_group_index]) / spread[prompt_group_index] / total
    incoming_gradient = coefficient[:, None] * cotangent.astype(jnp.float32)
    backward_gradient = jnp.dot(incoming_gradient, target_lowdim_matrix.T, precision=lax.Precision.HIGHEST).astype(jnp.bfloat16)
    left_factor_gradient = adapter_scale * jnp.dot(backward_gradient.T, hidden, preferred_element_type=jnp.float32)
    right_factor_gradient = adapter_scale * jnp.dot(rank_projection.T, incoming_gradient, precision=lax.Precision.HIGHEST)
    next_left_factor, next_first_moment_left, next_second_moment_left = adaptive_moment_step(source_lowdim_matrix, left_factor_gradient, running_mean_source_matrix, running_variance_source_matrix)
    next_right_factor, next_first_moment_right, next_second_moment_right = adaptive_moment_step(target_lowdim_matrix, right_factor_gradient, running_mean_target_matrix, running_variance_target_matrix)
    a_send = next_left_factor.astype(jnp.bfloat16)
    b_send = next_right_factor.astype(jnp.bfloat16)
    rows = INNER_NEURONS // N_TENSOR

    def merge_step(total_out, index):
        start = (index * rows).astype(jnp.int32)
        frozen_weight_block = lax.dynamic_slice_in_dim(frozen_down_weight, start, rows, 0)
        a_block = lax.dynamic_slice_in_dim(a_send, start, rows, 1)
        x_block = lax.dynamic_slice_in_dim(sampled_token_input, start, rows, 1)
        adapter_product = jnp.dot(a_block.T, b_send, preferred_element_type=jnp.float32)
        combined_weight = (frozen_weight_block.astype(jnp.float32) + adapter_scale * adapter_product).astype(jnp.bfloat16)
        return (total_out + jnp.dot(x_block, combined_weight, preferred_element_type=jnp.float32), None)
    start_total = jnp.zeros((sampled_token_input.shape[0], frozen_down_weight.shape[1]), jnp.float32)
    summed, _ = lax.scan(merge_step, start_total, jnp.arange(N_TENSOR, dtype=jnp.int32))
    rollout_out = summed.astype(jnp.bfloat16)
    return (rollout_out, next_left_factor, next_first_moment_left, next_second_moment_left, next_right_factor, next_first_moment_right, next_second_moment_right)
```

```python
import functools

import jax
import jax.numpy as jnp
from jax import lax
from jax.experimental import pallas as pl
from jax.experimental.pallas import tpu as pltpu
from jax.sharding import PartitionSpec as P

adapter_scale = 2.0
bias_one = 1.0 - 0.9**10
bias_two = 1.0 - 0.999**10

F32 = jnp.float32
BF16 = jnp.bfloat16
LANES = 128
MIB = 1 << 20


def dot(a, b):
    return jnp.dot(a, b, preferred_element_type=F32)


def dot_nt(a, b):
    length = a.shape[1]
    cut = length // 512 * 256
    if cut < 512:
        return dot_nt_part(a, b, 0, length)
    return dot_nt_part(a, b, 0, cut) + dot_nt_part(a, b, cut, length)


def dot_nt_part(a, b, first, last):
    dims = (((1,), (1,)), ((), ()))
    return lax.dot_general(a[:, first:last], b[:, first:last], dims, preferred_element_type=F32)


def adaptive_moment_step(param, grad, first, second):
    first = 0.9 * first + 0.1 * grad
    second = 0.999 * second + 0.001 * grad * grad
    param = param - 0.004 * (first / bias_one) / (jnp.sqrt(second / bias_two) + 1e-08)
    return (param, first, second)


def tile_of(length, limit):
    units = length // LANES
    return LANES * max(u for u in range(1, limit // LANES + 1) if units % u == 0)


def split_bf16(value):
    high = value.astype(BF16)
    return high, (value - high.astype(F32)).astype(BF16)


def pick(index, choices):
    result = choices[0]
    for at in range(1, len(choices)):
        result = jnp.where(index == at, choices[at], result)
    return result


def shape(dims, kind):
    return jax.ShapeDtypeStruct(dims, kind)


ANY = pl.BlockSpec(memory_space=pl.ANY)
HBM = pl.BlockSpec(memory_space=pltpu.HBM)
VMEM = pl.BlockSpec(memory_space=pltpu.VMEM)


def call(kernel, name, held, far, outputs, far_outputs, scratch, flops, vmem, after=()):
    first = len(held) + len(far)
    moved = sum(a.size * a.dtype.itemsize for a in [*far, *far_outputs])

    def body(*refs):
        kernel(*refs[:first], *refs[first + len(after) :])

    return pl.pallas_call(
        body,
        name=name,
        out_shape=[*outputs, *far_outputs],
        in_specs=[VMEM] * len(held) + [HBM] * len(far) + [ANY] * len(after),
        out_specs=[VMEM] * len(outputs) + [HBM] * len(far_outputs),
        scratch_shapes=scratch,
        compiler_params=pltpu.CompilerParams(vmem_limit_bytes=vmem * MIB),
        cost_estimate=pl.CostEstimate(flops=flops, bytes_accessed=moved, transcendentals=0),
    )(*held, *far, *after)


def in_turn(fetches, ahead=2):
    for fetch in fetches[:ahead]:
        fetch.start()
    done = []

    def arrive():
        fetches[len(done)].wait()
        done.append(True)
        if len(done) - 1 + ahead < len(fetches):
            fetches[len(done) - 1 + ahead].start()

    return arrive


def project_kernel(peers, part, index, mask, order, far_hidden, far_a, far_cot, far_b, pieces, stats, *rest):
    packed, hidden, a, cot, b, arrived = rest
    rank = a.shape[0]
    width = hidden.shape[2]
    chunks = hidden.shape[0]

    pairs = [(far_a, a)]
    pairs += [(far_hidden.at[:, at * width : (at + 1) * width], hidden.at[at]) for at in range(chunks)]
    pairs += [(far_cot, cot), (far_b, b)]
    fetches = [pltpu.make_async_copy(*pair, arrived.at[at]) for at, pair in enumerate(pairs)]
    arrive = in_turn(fetches, 3)
    arrive()
    left = a[...].astype(BF16)
    total = None
    for at in range(chunks):
        arrive()
        product = dot_nt(hidden.at[at], left[:, at * width : (at + 1) * width])
        total = product if total is None else total + product
    arrive()
    arrive()
    high, low = split_bf16(b[...])
    both = dot_nt(cot, jnp.concatenate([high, low], axis=0))
    packed[:, 0:rank] = total
    packed[:, rank : 2 * rank] = both[:, :rank] + both[:, rank:]
    for k in range(peers):
        block = packed[k * part : (k + 1) * part, :]
        pieces[k] = jnp.concatenate([block[: part // 2], block[part // 2 :]], axis=1)
    groups, tokens = stats.shape[1], index.shape[1]
    member = (lax.broadcasted_iota(jnp.int32, (groups, tokens), 0) == index[...]).astype(F32)
    row = lax.broadcasted_iota(jnp.int32, (8, tokens), 0)
    values = jnp.where(row == 0, mask[...], 0)
    values = jnp.where(row == 1, mask[...] * order[...], values)
    values = jnp.where(row == 2, mask[...] * order[...] * order[...], values)
    stats[...] = dot_nt(values.astype(F32).astype(BF16), member.astype(BF16))


def weigh_kernel(peers, rank, all_index, all_mask, all_order, pieces, *rest):
    stats, (out, column) = rest[:-2], rest[-2:]
    part, tokens = out.shape[1], all_index.shape[1]
    groups = stats[0].shape[1]
    sums = stats[0][...]
    for other in stats[1:]:
        sums = sums + other[...]
    counts, firsts, squares = sums[0:1, :], sums[1:2, :], sums[2:3, :]
    safe = jnp.maximum(counts, 1.0)
    mean = firsts / safe
    spread = jnp.maximum(jnp.sqrt(jnp.maximum(squares / safe - mean * mean, 0.0)), 1.0)
    total = jnp.maximum(jnp.sum(counts, axis=1, keepdims=True), 1.0)

    row = lax.broadcasted_iota(jnp.int32, (LANES, tokens), 0)
    tall = jnp.where(row == 0, all_index[...], 0)
    tall = jnp.where(row == 1, all_mask[...], tall)
    tall = jnp.where(row == 2, all_order[...], tall)
    column[...] = jnp.transpose(tall.astype(F32))
    own = column[pl.ds(pl.multiple_of(lax.axis_index("tensor") * part, part), part), :]
    index, mask, order = own[:, 0:1], own[:, 1:2], own[:, 2:3]
    member = index == lax.broadcasted_iota(jnp.int32, (part, groups), 1).astype(F32)
    own_mean = jnp.sum(jnp.where(member, mean, 0.0), axis=1, keepdims=True)
    own_spread = jnp.sum(jnp.where(member, spread, 0.0), axis=1, keepdims=True)
    coefficient = -mask * (order - own_mean) / own_spread / total

    both = pieces[0]
    for at in range(1, peers):
        both = both + pieces[at]
    both = jnp.concatenate([both[:, : 2 * rank], both[:, 2 * rank : 4 * rank]], axis=0)
    both = both * coefficient
    back = both[:, rank:].astype(BF16).astype(F32)
    high, low = split_bf16(both[:, :rank])
    whole = [back, high.astype(F32), low.astype(F32), jnp.zeros((part, LANES - 3 * rank), F32)]
    share = jnp.concatenate(whole, axis=1).astype(BF16)
    for at in range(peers):
        out[at] = share


def gradient_kernel(replicas, rank, shares, far_hidden, far_cot, own_a, own_b, *rest):
    sent, (grad, hidden, cot, arrived) = rest[:-4], rest[-4:]
    rows = rank // replicas
    half = grad.shape[1] // 2
    me = lax.axis_index("dp")
    chunks, high, _ = hidden.shape

    pairs = [(far_hidden.at[at * high : (at + 1) * high, :], hidden.at[at]) for at in range(chunks)]
    pairs.append((far_cot, cot))
    fetches = [pltpu.make_async_copy(*pair, arrived.at[at]) for at, pair in enumerate(pairs)]
    arrive = in_turn(fetches)
    tall = jnp.concatenate([shares[at] for at in range(shares.shape[0])], axis=0)
    wide = jnp.transpose(tall.astype(F32)).astype(BF16)
    for at in range(chunks):
        arrive()
        product = adapter_scale * dot(wide[0:rank, at * high : (at + 1) * high], hidden[at])
        if at == 0:
            grad[...] = product
        else:
            grad[...] += product
    arrive()
    both = dot(wide[rank : 3 * rank, :], cot[...])
    whole = adapter_scale * (both[:rank] + both[rank:])
    pieces = [grad[j * rows : (j + 1) * rows, :] for j in range(replicas)]
    own_a[...] = pick(me, pieces)
    own_b[...] = whole
    folded = [whole[at : at + 2 * rows] for at in range(0, rank, 2 * rows)]
    folded = jnp.concatenate(folded, axis=1).astype(BF16)
    for k in range(1, replicas):
        piece = pick(lax.bitwise_xor(me, k), pieces)
        halves = jnp.concatenate([piece[:, :half], piece[:, half:]], axis=0)
        sent[k - 1][:, 0:half] = halves.astype(BF16)
        sent[k - 1][:, half:] = folded


def update_kernel(replicas, own_a, own_b, x, *rest):
    received, rest = rest[: replicas - 1], rest[replicas - 1 :]
    factors, (sent, out), results = rest[:6], rest[6:8], rest[8:14]
    (a, am, av, b, bm, bv), made, arrived, left = rest[14:20], rest[20:26], rest[26], rest[27]
    rows, inner = a.shape
    rank, columns = b.shape
    me = lax.axis_index("dp")

    def fetch(at):
        source = factors[at]
        if at < 3 and source.shape[0] != rows:
            source = source.at[pl.ds(pl.multiple_of(me * rows, rows), rows), :]
        return pltpu.make_async_copy(source, (a, am, av, b, bm, bv)[at], arrived.at[at])

    def keep(at):
        return pltpu.make_async_copy(made[at], results[at], arrived.at[at])

    for at in range(6):
        fetch(at).start()
    grad_a, grad_b = own_a[...], own_b[...]
    half = inner // 2
    for other in received:
        folded = other[...].astype(F32)
        grad_a = grad_a + jnp.concatenate([folded[:rows, :half], folded[rows:, :half]], axis=1)
        parts = [folded[:, at : at + columns] for at in range(half, folded.shape[1], columns)]
        grad_b = grad_b + jnp.concatenate(parts, axis=0)
    for at in range(6):
        fetch(at).wait()
    made[0][...], made[1][...], made[2][...] = adaptive_moment_step(a[...], grad_a, am[...], av[...])
    padding = jnp.zeros((left.shape[0] - rows, inner), F32)
    left[...] = jnp.concatenate([made[0][...], padding], axis=0).astype(BF16)
    next_b, first_b, second_b = adaptive_moment_step(b[...], grad_b, bm[...], bv[...])
    for array, result in zip((next_b, first_b, second_b), made[3:]):
        result[...] = pick(me, [array[j * rows : (j + 1) * rows] for j in range(replicas)])
    for at in range(6):
        keep(at).start()
    width = columns // replicas
    choices = [next_b[:, j * width : (j + 1) * width] for j in range(replicas)]
    sent[...] = pick(me, choices).astype(BF16)
    product = dot_nt(x, left)
    empty = jnp.zeros((product.shape[0], LANES - left.shape[0]), F32)
    product = jnp.transpose(jnp.concatenate([product, empty], axis=1))[0:rows, :]
    for at in range(out.shape[0]):
        out[at] = product
    for at in range(6):
        keep(at).wait()


def rollout_kernel(jobs, following, given, x, *rest):
    first = rest[0] if given else None
    w, *outs = rest[given:-2]
    held, arrived = rest[-2:]
    after = outs.pop() if following else None
    _, inner, tile = held.shape
    width = outs[0].shape[1]
    tiles = width // tile
    me = lax.axis_index("tensor")
    todo = [(job, at) for job in range(len(jobs)) for at in range(tiles)]

    def columns(job, at):
        differs, other = job
        device = lax.bitwise_xor(me, 2 * differs + other)
        return w.at[:, pl.ds(pl.multiple_of(device * width + at * tile, tile), tile)]

    fetches, blocks = [], [first] if given else []
    for number in range(len(blocks), len(todo)):
        job, at = todo[number]
        slot = number - given
        blocks.append(held.at[slot])
        fetches.append(pltpu.make_async_copy(columns(jobs[job], at), held.at[slot], arrived.at[slot]))
    if following:
        fetches.append(pltpu.make_async_copy(columns(following, 0), after, arrived.at[len(fetches)]))
    arrive = in_turn(fetches)
    cut = x.shape[0] // 2
    for number, (job, at) in enumerate(todo):
        if number or not given:
            arrive()
        block = blocks[number]
        for rows in (slice(0, cut), slice(cut, 2 * cut)):
            product = dot(x[rows, :], block[...])
            outs[job][rows, at * tile : (at + 1) * tile] = product.astype(outs[job].dtype)
    if following:
        arrive()


def join_kernel(*refs):
    total = refs[0][...].astype(F32)
    for leaf in refs[1:-1]:
        total = total + leaf[...].astype(F32)
    refs[-1][...] = total.astype(refs[-1].dtype)


def finish_kernel(replicas, peers, rank, factor, *rest):
    products, leaves, (out, made, kept) = rest[:replicas], rest[replicas:-3], rest[-3:]
    me = lax.axis_index("dp")
    held = [p[...] for p in products]
    product = [pick(lax.bitwise_xor(me, r), held) for r in range(replicas)]
    high, low = split_bf16(jnp.concatenate(product, axis=0))
    empty = jnp.zeros((LANES - 2 * rank, high.shape[1]), F32)
    wide = jnp.concatenate([high.astype(F32), low.astype(F32), empty], axis=0)
    tall = jnp.transpose(wide).astype(BF16)
    empty = jnp.zeros((LANES - 2 * rank, factor.shape[1]), BF16)
    total = adapter_scale * dot(tall, jnp.concatenate([factor[...], factor[...], empty], axis=0))
    for leaf in leaves:
        total = total + leaf[...].astype(F32)
    made[...] = total.astype(BF16)
    copy = pltpu.make_async_copy(made, out, kept)
    copy.start()
    copy.wait()


def shards(
    hidden,
    cotangent,
    prompt_group_index,
    answer_token_mask,
    token_reward_order,
    source_lowdim_matrix,
    running_mean_source_matrix,
    running_variance_source_matrix,
    target_lowdim_matrix,
    running_mean_target_matrix,
    running_variance_target_matrix,
    frozen_down_weight,
    sampled_token_input,
):
    replicas, peers = lax.axis_size("dp"), lax.axis_size("tensor")
    me_dp = lax.axis_index("dp")
    x, w = sampled_token_input, frozen_down_weight
    tokens, inner = hidden.shape
    columns = cotangent.shape[1]
    rank = source_lowdim_matrix.shape[0]
    rows = rank // replicas
    part = tokens // peers
    groups = tokens * replicas // 8
    rollout = x.shape[0]
    own_width = w.shape[1] // peers
    deep = tile_of(inner, 1664)

    def xor(array, k, axis="tensor"):
        return lax.ppermute(array, axis, [(i, i ^ k) for i in range(lax.axis_size(axis))])

    tok = [
        array.reshape(1, tokens) for array in (prompt_group_index, answer_token_mask, token_reward_order)
    ]
    pieces, stats = call(
        functools.partial(project_kernel, peers, part),
        "project",
        tok,
        [hidden, source_lowdim_matrix, cotangent, target_lowdim_matrix],
        [shape((peers, part // 2, LANES), F32), shape((8, groups), F32)],
        [],
        [
            pltpu.VMEM((tokens, 2 * rank), F32),
            pltpu.VMEM((inner // deep, tokens, deep), BF16),
            pltpu.VMEM((rank, inner), F32),
            pltpu.VMEM((tokens, columns), BF16),
            pltpu.VMEM((rank, columns), F32),
            pltpu.SemaphoreType.DMA((inner // deep + 3,)),
        ],
        2 * tokens * (inner + columns) * 256,
        54,
    )
    all_stats = [stats] + [xor(stats, k, "dp") for k in range(1, replicas)]
    pieces = lax.all_to_all(pieces, "tensor", 0, 0)

    (share,) = call(
        functools.partial(weigh_kernel, peers, rank),
        "weigh",
        [*tok, pieces, *all_stats],
        [],
        [shape((peers, part, LANES), BF16)],
        [],
        [pltpu.VMEM((tokens, LANES), F32)],
        2 * part * groups,
        16,
    )
    shares = lax.all_to_all(share, "tensor", 0, 0)

    chips = peers // 2
    tile = min(own_width, 256)
    crossed, arrived, leaves, handed = {}, {}, [], None

    def form(jobs, following, after, held_up=()):
        nonlocal handed, leaves
        given = handed is not None
        results = [shape((rollout, own_width), BF16 if other else F32) for _, other in jobs]
        slots = len(jobs) * own_width // tile - given
        if following:
            results.append(shape((inner, tile), BF16))
        *results, last = call(
            functools.partial(rollout_kernel, jobs, following, given),
            "rollout%d" % jobs[0][0],
            [x, handed] if given else [x],
            [w],
            results,
            [],
            [
                pltpu.VMEM((max(slots, 1), inner, tile), BF16),
                pltpu.SemaphoreType.DMA((slots + 1,)),
            ],
            2 * rollout * inner * own_width * len(jobs),
            34,
            after,
        )
        handed = last if following else None
        if not following:
            results.append(last)
        for (m, other), result in zip(jobs, results):
            if other:
                crossed[m] = xor(result, 1)
        for (m, other), result in zip(jobs, results):
            if other:
                continue
            leaves = [result, crossed[m]]
            bit = 1
            while bit < chips and not m & bit:
                leaves.append(arrived[m | bit])
                bit *= 2
            if m:
                joined = shape((rollout, own_width), BF16)
                (result,) = call(join_kernel, "join", leaves, [], [joined], [], [], 0, 8, held_up)
                arrived[m] = xor(result, 2 * bit)
            last = result
        return last

    half = chips // 2
    before = form([(chips - 1, 1), (chips - 1, 0), (chips - 2, 1)], None, [share], [shares])
    for m in range(chips - 2, half, -1):
        before = form([(m, 0), (m - 1, 1)], None, [before])

    own_a, own_b, *sent = call(
        functools.partial(gradient_kernel, replicas, rank),
        "gradient",
        [shares],
        [hidden, cotangent],
        [shape((rows, inner), F32), shape((rank, columns), F32)]
        + [shape((2 * rows, inner // 2 + columns * replicas // 2), BF16)] * (replicas - 1),
        [],
        [
            pltpu.VMEM((rank, inner), F32),
            pltpu.VMEM((4, tokens // 4, inner), BF16),
            pltpu.VMEM((tokens, columns), BF16),
            pltpu.SemaphoreType.DMA((5,)),
        ],
        2 * tokens * (inner + columns) * 256,
        54,
        [before],
    )
    received = [xor(array, k + 1, "dp") for k, array in enumerate(sent)]
    before = form([(half, 0), (half - 1, 1)], (half - 1, 0), [own_a])

    left = [source_lowdim_matrix, running_mean_source_matrix, running_variance_source_matrix]
    right = [target_lowdim_matrix, running_mean_target_matrix, running_variance_target_matrix]
    if rows % 8:
        left = [lax.dynamic_slice_in_dim(array, me_dp * rows, rows, 0) for array in left]
    own_left, own_right = shape((rows, inner), F32), shape((rows, columns), F32)
    sent_b, product, *updated = call(
        functools.partial(update_kernel, replicas),
        "update",
        [own_a, own_b, x, *received],
        [*left, *right],
        [shape((rank, columns // replicas), BF16), shape((peers, rows, rollout), F32)],
        [own_left] * 3 + [own_right] * 3,
        [pltpu.VMEM((rows, inner), F32)] * 3
        + [pltpu.VMEM((rank, columns), F32)] * 3
        + [pltpu.VMEM((rows, inner), F32)] * 3
        + [pltpu.VMEM((rows, columns), F32)] * 3
        + [pltpu.SemaphoreType.DMA((6,)), pltpu.VMEM((16, inner), BF16)],
        2 * rollout * inner * 256,
        28,
        [before],
    )
    pairs = [(dp * peers + at, at * replicas + dp) for dp in range(replicas) for at in range(peers)]
    factor = lax.ppermute(sent_b, ("dp", "tensor"), pairs)
    for m in range(half - 1, -1, -1):
        jobs = [(m, 0), (m - 1, 1)] if m else [(0, 0)]
        before = form(jobs, (m - 1, 0) if m else None, [before, product])
    product = jnp.sum(lax.all_to_all(product, "tensor", 0, 0), axis=0)
    products = [product] + [xor(product, k, "dp") for k in range(1, replicas)]

    (result,) = call(
        functools.partial(finish_kernel, replicas, peers, rank),
        "finish",
        [factor, *products, *leaves],
        [],
        [],
        [shape((rollout, own_width), BF16)],
        [pltpu.VMEM((rollout, own_width), BF16), pltpu.SemaphoreType.DMA(())],
        2 * rollout * own_width * 256,
        16,
    )
    return (result, *updated)


def solution(mesh):
    placed = (
        P("dp", "tensor"),
        P("dp", "tensor"),
        P("dp"),
        P("dp"),
        P("dp"),
        P(None, "tensor"),
        P(None, "tensor"),
        P(None, "tensor"),
        P(None, "tensor"),
        P(None, "tensor"),
        P(None, "tensor"),
        P("tensor", "dp"),
        P(None, "tensor"),
    )
    return jax.shard_map(
        shards,
        mesh=mesh,
        in_specs=placed,
        out_specs=(P(None, ("dp", "tensor")), *[P("dp", "tensor")] * 6),
        check_vma=False,
    )
```

```python
import functools

import jax
import jax.numpy as jnp
from jax import lax
from jax.experimental import pallas as pl
from jax.experimental.pallas import tpu as pltpu
from jax.sharding import PartitionSpec as P

adapter_scale = 2.0
bias_one = 1.0 - 0.9**10
bias_two = 1.0 - 0.999**10

F32 = jnp.float32
BF16 = jnp.bfloat16
LANES = 128
MIB = 1 << 20


def dot(a, b):
    return jnp.dot(a, b, preferred_element_type=F32)


def dot_nt(a, b):
    length = a.shape[1]
    cut = length // 512 * 256
    if cut < 512:
        return dot_nt_part(a, b, 0, length)
    return dot_nt_part(a, b, 0, cut) + dot_nt_part(a, b, cut, length)


def dot_nt_part(a, b, first, last):
    dims = (((1,), (1,)), ((), ()))
    return lax.dot_general(a[:, first:last], b[:, first:last], dims, preferred_element_type=F32)


def adaptive_moment_step(param, grad, first, second):
    first = 0.9 * first + 0.1 * grad
    second = 0.999 * second + 0.001 * grad * grad
    param = param - 0.004 * (first / bias_one) / (jnp.sqrt(second / bias_two) + 1e-08)
    return (param, first, second)


def tile_of(length, limit):
    units = length // LANES
    return LANES * max(u for u in range(1, limit // LANES + 1) if units % u == 0)


def split_bf16(value):
    high = value.astype(BF16)
    return high, (value - high.astype(F32)).astype(BF16)


def pick(index, choices):
    result = choices[0]
    for at in range(1, len(choices)):
        result = jnp.where(index == at, choices[at], result)
    return result


def shape(dims, kind):
    return jax.ShapeDtypeStruct(dims, kind)


ANY = pl.BlockSpec(memory_space=pl.ANY)
HBM = pl.BlockSpec(memory_space=pltpu.HBM)
VMEM = pl.BlockSpec(memory_space=pltpu.VMEM)


def call(kernel, name, held, far, outputs, far_outputs, scratch, flops, vmem, after=()):
    first = len(held) + len(far)
    moved = sum(a.size * a.dtype.itemsize for a in [*far, *far_outputs])

    def body(*refs):
        kernel(*refs[:first], *refs[first + len(after) :])

    return pl.pallas_call(
        body,
        name=name,
        out_shape=[*outputs, *far_outputs],
        in_specs=[VMEM] * len(held) + [HBM] * len(far) + [ANY] * len(after),
        out_specs=[VMEM] * len(outputs) + [HBM] * len(far_outputs),
        scratch_shapes=scratch,
        compiler_params=pltpu.CompilerParams(vmem_limit_bytes=vmem * MIB),
        cost_estimate=pl.CostEstimate(flops=flops, bytes_accessed=moved, transcendentals=0),
    )(*held, *far, *after)


def in_turn(fetches, ahead=2):
    for fetch in fetches[:ahead]:
        fetch.start()
    done = []

    def arrive():
        fetches[len(done)].wait()
        done.append(True)
        if len(done) - 1 + ahead < len(fetches):
            fetches[len(done) - 1 + ahead].start()

    return arrive


def project_kernel(index, mask, order, far_hidden, far_a, far_cot, far_b, far_x, *rest):
    packed, stats, hidden, cot, x, a, b, arrived = rest
    rank = a.shape[0]
    inner = hidden.shape[1]
    chunks = arrived.shape[0] - 4
    width = inner // chunks
    pairs = [(far_a, a)]
    for at in range(chunks):
        columns = slice(at * width, (at + 1) * width)
        pairs.append((far_hidden.at[:, columns], hidden.at[:, columns]))
    pairs += [(far_cot, cot), (far_b, b), (far_x, x)]
    fetches = [pltpu.make_async_copy(*pair, arrived.at[at]) for at, pair in enumerate(pairs)]
    arrive = in_turn(fetches, 3)
    arrive()
    left = a[...].astype(BF16)
    total = None
    for at in range(chunks):
        arrive()
        columns = slice(at * width, (at + 1) * width)
        product = dot_nt(hidden.at[:, columns], left[:, columns])
        total = product if total is None else total + product
    arrive()
    arrive()
    high, low = split_bf16(b[...])
    both = dot_nt(cot, jnp.concatenate([high, low], axis=0))
    both = jnp.concatenate([total, both[:, :rank] + both[:, rank:]], axis=1)
    half = both.shape[0] // 2
    packed[...] = jnp.concatenate([both[:half], both[half:]], axis=1)
    groups, tokens = stats.shape[1], index.shape[1]
    member = (lax.broadcasted_iota(jnp.int32, (groups, tokens), 0) == index[...]).astype(F32)
    row = lax.broadcasted_iota(jnp.int32, (8, tokens), 0)
    values = jnp.where(row == 0, mask[...], 0)
    values = jnp.where(row == 1, mask[...] * order[...], values)
    values = jnp.where(row == 2, mask[...] * order[...] * order[...], values)
    stats[...] = dot_nt(values.astype(F32).astype(BF16), member.astype(BF16))
    arrive()


def gradient_kernel(replicas, rank, all_index, all_mask, all_order, packed, arrived, hidden, cot, *rest):
    stats, (own_a, own_b, *sent) = rest[:replicas], rest[replicas:-2]
    column, grad = rest[-2:]
    rows = rank // replicas
    me = lax.axis_index("dp")
    tokens, inner = hidden.shape
    groups = stats[0].shape[1]
    half = inner // 2
    sums = stats[0][...]
    for other in stats[1:]:
        sums = sums + other[...]
    counts, firsts, squares = sums[0:1, :], sums[1:2, :], sums[2:3, :]
    safe = jnp.maximum(counts, 1.0)
    mean = firsts / safe
    spread = jnp.maximum(jnp.sqrt(jnp.maximum(squares / safe - mean * mean, 0.0)), 1.0)
    total = jnp.maximum(jnp.sum(counts, axis=1, keepdims=True), 1.0)

    row = lax.broadcasted_iota(jnp.int32, (LANES, tokens), 0)
    tall = jnp.where(row == 0, all_index[...], 0)
    tall = jnp.where(row == 1, all_mask[...], tall)
    tall = jnp.where(row == 2, all_order[...], tall)
    column[...] = jnp.transpose(tall.astype(F32))
    index, mask, order = column[:, 0:1], column[:, 1:2], column[:, 2:3]
    member = index == lax.broadcasted_iota(jnp.int32, (tokens, groups), 1).astype(F32)
    own_mean = jnp.sum(jnp.where(member, mean, 0.0), axis=1, keepdims=True)
    own_spread = jnp.sum(jnp.where(member, spread, 0.0), axis=1, keepdims=True)
    coefficient = -mask * (order - own_mean) / own_spread / total

    both = packed[...] + arrived[...]
    both = jnp.concatenate([both[:, : 2 * rank], both[:, 2 * rank : 4 * rank]], axis=0)
    both = both * coefficient
    back = both[:, rank:].astype(BF16).astype(F32)
    high, low = split_bf16(both[:, :rank])
    empty = jnp.zeros((tokens, LANES - 3 * rank), F32)
    tall = jnp.concatenate([back, high.astype(F32), low.astype(F32), empty], axis=1)
    wide = jnp.transpose(tall).astype(BF16)
    grad[...] = adapter_scale * dot(wide[0:rank, :], hidden[...])
    both = dot(wide[rank : 3 * rank, :], cot[...])
    whole = adapter_scale * (both[:rank] + both[rank:])
    pieces = [grad[j * rows : (j + 1) * rows, :] for j in range(replicas)]
    own_a[...] = pick(me, pieces)
    own_b[...] = whole
    folded = [whole[at : at + 2 * rows] for at in range(0, rank, 2 * rows)]
    folded = jnp.concatenate(folded, axis=1).astype(BF16)
    for k in range(1, replicas):
        piece = pick(lax.bitwise_xor(me, k), pieces)
        halves = jnp.concatenate([piece[:, :half], piece[:, half:]], axis=0)
        sent[k - 1][:, 0:half] = halves.astype(BF16)
        sent[k - 1][:, half:] = folded


def update_kernel(replicas, own_a, own_b, x, *rest):
    received, rest = rest[: replicas - 1], rest[replicas - 1 :]
    factors, (sent, out), results = rest[:6], rest[6:8], rest[8:14]
    (a, am, av, b, bm, bv), made, arrived, left = rest[14:20], rest[20:26], rest[26], rest[27]
    rows, inner = a.shape
    rank, columns = b.shape
    me = lax.axis_index("dp")

    def fetch(at):
        source = factors[at]
        if at < 3 and source.shape[0] != rows:
            source = source.at[pl.ds(pl.multiple_of(me * rows, rows), rows), :]
        return pltpu.make_async_copy(source, (a, am, av, b, bm, bv)[at], arrived.at[at])

    def keep(at):
        return pltpu.make_async_copy(made[at], results[at], arrived.at[at])

    for at in range(6):
        fetch(at).start()
    grad_a, grad_b = own_a[...], own_b[...]
    half = inner // 2
    for other in received:
        folded = other[...].astype(F32)
        grad_a = grad_a + jnp.concatenate([folded[:rows, :half], folded[rows:, :half]], axis=1)
        parts = [folded[:, at : at + columns] for at in range(half, folded.shape[1], columns)]
        grad_b = grad_b + jnp.concatenate(parts, axis=0)
    for at in range(6):
        fetch(at).wait()
    made[0][...], made[1][...], made[2][...] = adaptive_moment_step(a[...], grad_a, am[...], av[...])
    padding = jnp.zeros((left.shape[0] - rows, inner), F32)
    left[...] = jnp.concatenate([made[0][...], padding], axis=0).astype(BF16)
    next_b, first_b, second_b = adaptive_moment_step(b[...], grad_b, bm[...], bv[...])
    for array, result in zip((next_b, first_b, second_b), made[3:]):
        result[...] = pick(me, [array[j * rows : (j + 1) * rows] for j in range(replicas)])
    for at in range(6):
        keep(at).start()
    width = columns // replicas
    choices = [next_b[:, j * width : (j + 1) * width] for j in range(replicas)]
    sent[...] = pick(me, choices).astype(BF16)
    product = dot_nt(x, left)
    empty = jnp.zeros((product.shape[0], LANES - left.shape[0]), F32)
    out[...] = jnp.transpose(jnp.concatenate([product, empty], axis=1))[0:rows, :]
    for at in range(6):
        keep(at).wait()


def rollout_kernel(differs, following, first, x, *rest):
    if following is None:
        given, out = rest
    elif first:
        w, out, after, given, arrived = rest
    else:
        given, w, out, after, arrived = rest
    me = lax.axis_index("tensor")
    width = out.shape[1]

    def fetch(differs, held, at):
        start = pl.multiple_of(lax.bitwise_xor(me, differs) * width, width)
        return pltpu.make_async_copy(w.at[:, pl.ds(start, width)], held, arrived.at[at])

    if first:
        own = fetch(differs, given, 0)
        own.start()
        own.wait()
    if following is not None:
        next_one = fetch(following, after, 1)
        next_one.start()
    out[...] = dot(x[...], given[...]).astype(out.dtype)
    if following is not None:
        next_one.wait()


def gather_kernel(bit, mine, arrived, out):
    later = lax.bitwise_and(lax.shift_right_logical(lax.axis_index("dp"), bit), 1) == 1
    first = jnp.where(later, arrived[...], mine[...])
    out[...] = jnp.concatenate([first, jnp.where(later, mine[...], arrived[...])], axis=0)


def join_kernel(*refs):
    total = refs[0][...].astype(F32)
    for leaf in refs[1:-1]:
        total = total + leaf[...].astype(F32)
    refs[-1][...] = total.astype(refs[-1].dtype)


def finish_kernel(rank, factor, mine, arrived, *rest):
    leaves, (out, made, kept) = rest[:-3], rest[-3:]
    high, low = split_bf16(mine[...] + arrived[...])
    empty = jnp.zeros((LANES - 2 * rank, high.shape[1]), F32)
    wide = jnp.concatenate([high.astype(F32), low.astype(F32), empty], axis=0)
    tall = jnp.transpose(wide).astype(BF16)
    empty = jnp.zeros((LANES - 2 * rank, factor.shape[1]), BF16)
    total = adapter_scale * dot(tall, jnp.concatenate([factor[...], factor[...], empty], axis=0))
    for leaf in leaves:
        total = total + leaf[...].astype(F32)
    made[...] = total.astype(BF16)
    copy = pltpu.make_async_copy(made, out, kept)
    copy.start()
    copy.wait()


def shards(
    hidden,
    cotangent,
    prompt_group_index,
    answer_token_mask,
    token_reward_order,
    source_lowdim_matrix,
    running_mean_source_matrix,
    running_variance_source_matrix,
    target_lowdim_matrix,
    running_mean_target_matrix,
    running_variance_target_matrix,
    frozen_down_weight,
    sampled_token_input,
):
    replicas, peers = lax.axis_size("dp"), lax.axis_size("tensor")
    me_dp = lax.axis_index("dp")
    x, w = sampled_token_input, frozen_down_weight
    tokens, inner = hidden.shape
    columns = cotangent.shape[1]
    rank = source_lowdim_matrix.shape[0]
    rows = rank // replicas
    groups = tokens * replicas // 8
    rollout = x.shape[0]
    own_width = w.shape[1] // peers
    deep = tile_of(inner, 1664)

    def xor(array, k, axis="tensor"):
        return lax.ppermute(array, axis, [(i, i ^ k) for i in range(lax.axis_size(axis))])

    def add(arrays, after=()):
        (total,) = call(
            join_kernel, "join", arrays, [], [shape(arrays[0].shape, arrays[-1].dtype)], [], [], 0, 8, after
        )
        return total

    chips = peers // 2
    todo = [(m, other) for m in range(chips - 1, -1, -1) for other in (1, 0)]
    crossed, arrived, own, waiting, handed = {}, {}, {}, [], None

    def form(eighths, after):
        nonlocal handed
        for _ in range(eighths * len(todo_all) // 8):
            m, other = todo.pop(0)
            following = 2 * todo[0][0] + todo[0][1] if todo else None
            result = shape((rollout, own_width), BF16 if other else F32)
            block = shape((inner, own_width), BF16)
            held = [x_held] if handed is None else [x_held, handed]
            scratch = [pltpu.VMEM(block.shape, BF16)] if handed is None else []
            scratch += [pltpu.SemaphoreType.DMA((2,))] if following is not None else []
            result, *handed = call(
                functools.partial(rollout_kernel, 2 * m + other, following, handed is None),
                "rollout%d%d" % (m, other),
                held,
                [w] if following is not None else [],
                [result] + ([block] if following is not None else []),
                [],
                scratch,
                2 * rollout * inner * own_width,
                20,
                after,
            )
            handed = handed[0] if handed else None
            if other:
                crossed[m] = xor(result, 1)
            else:
                own[m] = result
                waiting.append(m)
            after = [result]
        return after

    def leaves_of(m):
        bits = [1 << at for at in range(chips.bit_length() - 1)]
        lower = [bit for bit in bits if not m or bit < m & -m]
        return [own[m], crossed[m], *[arrived[m | bit] for bit in lower]]

    def send_on(after):
        while waiting:
            m = waiting.pop(0)
            total = add(leaves_of(m), after)
            arrived[m] = xor(total, 2 * (m & -m))
            after = [total]
        return after

    todo_all = list(todo)

    tok = [
        array.reshape(1, tokens) for array in (prompt_group_index, answer_token_mask, token_reward_order)
    ]
    packed, stats, hidden_held, cot_held, x_held = call(
        project_kernel,
        "project",
        tok,
        [hidden, source_lowdim_matrix, cotangent, target_lowdim_matrix, x],
        [
            shape((tokens // 2, LANES), F32),
            shape((8, groups), F32),
            shape(hidden.shape, BF16),
            shape(cotangent.shape, BF16),
            shape(x.shape, BF16),
        ],
        [],
        [
            pltpu.VMEM((rank, inner), F32),
            pltpu.VMEM((rank, columns), F32),
            pltpu.SemaphoreType.DMA((inner // deep + 4,)),
        ],
        2 * tokens * (inner + columns) * 256,
        45,
    )
    all_stats = [stats] + [xor(stats, k, "dp") for k in range(1, replicas)]
    tensor_bits = [1 << at for at in range(peers.bit_length() - 1)]
    received = xor(packed, tensor_bits[0])
    after = form(1, [packed])
    for bit in tensor_bits[1:]:
        packed = add([packed, received], after)
        received = xor(packed, bit)
        after = form(1, [packed]) if bit in (2, 4) else [packed]
    after = send_on(after)

    own_a, own_b, *sent = call(
        functools.partial(gradient_kernel, replicas, rank),
        "gradient",
        [*tok, packed, received, hidden_held, cot_held, *all_stats],
        [],
        [shape((rows, inner), F32), shape((rank, columns), F32)]
        + [shape((2 * rows, inner // 2 + columns * replicas // 2), BF16)] * (replicas - 1),
        [],
        [pltpu.VMEM((tokens, LANES), F32), pltpu.VMEM((rank, inner), F32)],
        2 * tokens * (inner + columns) * 256,
        16,
        after,
    )
    received = [xor(array, k + 1, "dp") for k, array in enumerate(sent)]
    after = form(1, send_on(form(1, [own_a])))

    left = [source_lowdim_matrix, running_mean_source_matrix, running_variance_source_matrix]
    right = [target_lowdim_matrix, running_mean_target_matrix, running_variance_target_matrix]
    if rows % 8:
        left = [lax.dynamic_slice_in_dim(array, me_dp * rows, rows, 0) for array in left]
    own_left, own_right = shape((rows, inner), F32), shape((rows, columns), F32)
    sent_b, product, *updated = call(
        functools.partial(update_kernel, replicas),
        "update",
        [own_a, own_b, x_held, *received],
        [*left, *right],
        [shape((rank, columns // replicas), BF16), shape((rows, rollout), F32)],
        [own_left] * 3 + [own_right] * 3,
        [pltpu.VMEM((rows, inner), F32)] * 3
        + [pltpu.VMEM((rank, columns), F32)] * 3
        + [pltpu.VMEM((rows, inner), F32)] * 3
        + [pltpu.VMEM((rows, columns), F32)] * 3
        + [pltpu.SemaphoreType.DMA((6,)), pltpu.VMEM((16, inner), BF16)],
        2 * rollout * inner * 256,
        24,
        after,
    )
    pairs = [(dp * peers + at, at * replicas + dp) for dp in range(replicas) for at in range(peers)]
    factor = lax.ppermute(sent_b, ("dp", "tensor"), pairs)
    after = [product]
    for at in range(replicas.bit_length() - 1):
        received = xor(product, 1 << at, "dp")
        if at < 2:
            after = form(1, after) if todo else after
        both = shape((2 * product.shape[0], rollout), F32)
        (product,) = call(
            functools.partial(gather_kernel, at), "gather", [product, received], [], [both], [], [], 0, 8, after
        )
        after = [product]
        if at < 1:
            after = send_on(after)
    for at, bit in enumerate(tensor_bits):
        received = xor(product, bit)
        if at == 0 and todo:
            after = form(len(todo) * 8 // len(todo_all), after)
        if at < len(tensor_bits) - 1:
            product = add([product, received], after + [factor] * (at == len(tensor_bits) - 2))
            after = [product]
    send_on_last = [m for m in waiting if m]
    waiting[:] = send_on_last
    send_on(after)

    (result,) = call(
        functools.partial(finish_kernel, rank),
        "finish",
        [factor, product, received, *leaves_of(0)],
        [],
        [],
        [shape((rollout, own_width), BF16)],
        [pltpu.VMEM((rollout, own_width), BF16), pltpu.SemaphoreType.DMA(())],
        2 * rollout * own_width * 256,
        16,
    )
    return (result, *updated)


def solution(mesh):
    placed = (
        P("dp", "tensor"),
        P("dp", "tensor"),
        P("dp"),
        P("dp"),
        P("dp"),
        P(None, "tensor"),
        P(None, "tensor"),
        P(None, "tensor"),
        P(None, "tensor"),
        P(None, "tensor"),
        P(None, "tensor"),
        P("tensor", "dp"),
        P(None, "tensor"),
    )
    return jax.shard_map(
        shards,
        mesh=mesh,
        in_specs=placed,
        out_specs=(P(None, ("dp", "tensor")), *[P("dp", "tensor")] * 6),
        check_vma=False,
    )
```

```python
import functools

import jax
import jax.numpy as jnp
from jax import lax
from jax.experimental import pallas as pl
from jax.experimental.pallas import tpu as pltpu
from jax.sharding import PartitionSpec as P

adapter_scale = 2.0
bias_one = 1.0 - 0.9**10
bias_two = 1.0 - 0.999**10

F32 = jnp.float32
BF16 = jnp.bfloat16
LANES = 128
MIB = 1 << 20


def dot(a, b):
    return jnp.dot(a, b, preferred_element_type=F32)


def dot_nt(a, b):
    length = a.shape[1]
    cut = length // 512 * 256
    if cut < 512:
        return dot_nt_part(a, b, 0, length)
    return dot_nt_part(a, b, 0, cut) + dot_nt_part(a, b, cut, length)


def dot_nt_part(a, b, first, last):
    dims = (((1,), (1,)), ((), ()))
    return lax.dot_general(a[:, first:last], b[:, first:last], dims, preferred_element_type=F32)


def adaptive_moment_step(param, grad, first, second):
    first = 0.9 * first + 0.1 * grad
    second = 0.999 * second + 0.001 * grad * grad
    param = param - 0.004 * (first / bias_one) / (jnp.sqrt(second / bias_two) + 1e-08)
    return (param, first, second)


def tile_of(length, limit):
    units = length // LANES
    return LANES * max(u for u in range(1, limit // LANES + 1) if units % u == 0)


def split_bf16(value):
    high = value.astype(BF16)
    return high, (value - high.astype(F32)).astype(BF16)


def pick(index, choices):
    result = choices[0]
    for at in range(1, len(choices)):
        result = jnp.where(index == at, choices[at], result)
    return result


def shape(dims, kind):
    return jax.ShapeDtypeStruct(dims, kind)


ANY = pl.BlockSpec(memory_space=pl.ANY)
HBM = pl.BlockSpec(memory_space=pltpu.HBM)
VMEM = pl.BlockSpec(memory_space=pltpu.VMEM)


def call(kernel, name, held, far, outputs, far_outputs, scratch, flops, vmem, after=()):
    first = len(held) + len(far)
    moved = sum(a.size * a.dtype.itemsize for a in [*far, *far_outputs])

    def body(*refs):
        kernel(*refs[:first], *refs[first + len(after) :])

    return pl.pallas_call(
        body,
        name=name,
        out_shape=[*outputs, *far_outputs],
        in_specs=[VMEM] * len(held) + [HBM] * len(far) + [ANY] * len(after),
        out_specs=[VMEM] * len(outputs) + [HBM] * len(far_outputs),
        scratch_shapes=scratch,
        compiler_params=pltpu.CompilerParams(vmem_limit_bytes=int(vmem * MIB)),
        cost_estimate=pl.CostEstimate(flops=flops, bytes_accessed=moved, transcendentals=0),
    )(*held, *far, *after)


def in_turn(fetches, ahead=2):
    for fetch in fetches[:ahead]:
        fetch.start()
    done = []

    def arrive():
        fetches[len(done)].wait()
        done.append(True)
        if len(done) - 1 + ahead < len(fetches):
            fetches[len(done) - 1 + ahead].start()

    return arrive


def project_kernel(differs, *rest):
    far_tok, (far_hidden, far_a, far_cot, far_b, far_x, w) = rest[:3], rest[3:9]
    packed, stats, tok, hidden, cot, x, block, index, mask, order, a, b, arrived = rest[9:]
    rank = a.shape[0]
    inner = hidden.shape[1]
    chunks = arrived.shape[0] - 8
    width = inner // chunks
    start = lax.bitwise_xor(lax.axis_index("tensor"), differs) * block.shape[1]
    first = w.at[:, pl.ds(pl.multiple_of(start, block.shape[1]), block.shape[1])]
    pairs = [*zip(far_tok, (index, mask, order)), (far_a, a)]
    for at in range(chunks):
        columns = slice(at * width, (at + 1) * width)
        pairs.append((far_hidden.at[:, columns], hidden.at[:, columns]))
    pairs += [(far_cot, cot), (far_b, b), (first, block), (far_x, x)]
    fetches = [pltpu.make_async_copy(*pair, arrived.at[at]) for at, pair in enumerate(pairs)]
    arrive = in_turn(fetches, 6)
    for _ in range(4):
        arrive()
    left = a[...].astype(BF16)
    total = None
    for at in range(chunks):
        arrive()
        columns = slice(at * width, (at + 1) * width)
        product = dot_nt(hidden.at[:, columns], left[:, columns])
        total = product if total is None else total + product
    arrive()
    arrive()
    high, low = split_bf16(b[...])
    both = dot_nt(cot, jnp.concatenate([high, low], axis=0))
    both = jnp.concatenate([total, both[:, :rank] + both[:, rank:]], axis=1)
    half = both.shape[0] // 2
    packed[...] = jnp.concatenate([both[:half], both[half:]], axis=1)
    groups, tokens = stats.shape[1], index.shape[1]
    member = (lax.broadcasted_iota(jnp.int32, (groups, tokens), 0) == index[...]).astype(F32)
    row = lax.broadcasted_iota(jnp.int32, (8, tokens), 0)
    values = jnp.where(row == 0, mask[...], 0)
    values = jnp.where(row == 1, mask[...] * order[...], values)
    values = jnp.where(row == 2, mask[...] * order[...] * order[...], values)
    stats[...] = dot_nt(values.astype(F32).astype(BF16), member.astype(BF16))
    for at, array in enumerate((index, mask, order)):
        tok[at : at + 1, :] = array[...]
    arrive()
    arrive()


def gradient_kernel(replicas, rank, tok, packed, arrived, hidden, cot, *rest):
    stats, (own_a, own_b, *sent) = rest[:replicas], rest[replicas:-2]
    column, grad = rest[-2:]
    rows = rank // replicas
    me = lax.axis_index("dp")
    tokens, inner = hidden.shape
    groups = stats[0].shape[1]
    half = inner // 2
    sums = stats[0][...]
    for other in stats[1:]:
        sums = sums + other[...]
    counts, firsts, squares = sums[0:1, :], sums[1:2, :], sums[2:3, :]
    safe = jnp.maximum(counts, 1.0)
    mean = firsts / safe
    spread = jnp.maximum(jnp.sqrt(jnp.maximum(squares / safe - mean * mean, 0.0)), 1.0)
    total = jnp.maximum(jnp.sum(counts, axis=1, keepdims=True), 1.0)

    row = lax.broadcasted_iota(jnp.int32, (LANES, tokens), 0)
    tall = jnp.where(row == 0, tok[0:1, :], 0)
    tall = jnp.where(row == 1, tok[1:2, :], tall)
    tall = jnp.where(row == 2, tok[2:3, :], tall)
    column[...] = jnp.transpose(tall.astype(F32))
    index, mask, order = column[:, 0:1], column[:, 1:2], column[:, 2:3]
    member = index == lax.broadcasted_iota(jnp.int32, (tokens, groups), 1).astype(F32)
    own_mean = jnp.sum(jnp.where(member, mean, 0.0), axis=1, keepdims=True)
    own_spread = jnp.sum(jnp.where(member, spread, 0.0), axis=1, keepdims=True)
    coefficient = -mask * (order - own_mean) / own_spread / total

    both = packed[...] + arrived[...]
    both = jnp.concatenate([both[:, : 2 * rank], both[:, 2 * rank : 4 * rank]], axis=0)
    both = both * coefficient
    back = both[:, rank:].astype(BF16).astype(F32)
    high, low = split_bf16(both[:, :rank])
    empty = jnp.zeros((tokens, LANES - 3 * rank), F32)
    tall = jnp.concatenate([back, high.astype(F32), low.astype(F32), empty], axis=1)
    wide = jnp.transpose(tall).astype(BF16)
    grad[...] = adapter_scale * dot(wide[0:rank, :], hidden[...])
    both = dot(wide[rank : 3 * rank, :], cot[...])
    whole = adapter_scale * (both[:rank] + both[rank:])
    pieces = [grad[j * rows : (j + 1) * rows, :] for j in range(replicas)]
    own_a[...] = pick(me, pieces)
    own_b[...] = whole
    folded = [whole[at : at + 2 * rows] for at in range(0, rank, 2 * rows)]
    folded = jnp.concatenate(folded, axis=1).astype(BF16)
    for k in range(1, replicas):
        piece = pick(lax.bitwise_xor(me, k), pieces)
        halves = jnp.concatenate([piece[:, :half], piece[:, half:]], axis=0)
        sent[k - 1][:, 0:half] = halves.astype(BF16)
        sent[k - 1][:, half:] = folded


def update_kernel(replicas, own_a, own_b, x, *rest):
    received, rest = rest[: replicas - 1], rest[replicas - 1 :]
    factors, (sent, out), results = rest[:6], rest[6:8], rest[8:14]
    (a, am, av, b, bm, bv), made, arrived, left = rest[14:20], rest[20:26], rest[26], rest[27]
    rows, inner = a.shape
    rank, columns = b.shape
    me = lax.axis_index("dp")

    def fetch(at):
        source = factors[at]
        if at < 3 and source.shape[0] != rows:
            source = source.at[pl.ds(pl.multiple_of(me * rows, rows), rows), :]
        return pltpu.make_async_copy(source, (a, am, av, b, bm, bv)[at], arrived.at[at])

    def keep(at):
        return pltpu.make_async_copy(made[at], results[at], arrived.at[at])

    for at in range(6):
        fetch(at).start()
    grad_a, grad_b = own_a[...], own_b[...]
    half = inner // 2
    for other in received:
        folded = other[...].astype(F32)
        grad_a = grad_a + jnp.concatenate([folded[:rows, :half], folded[rows:, :half]], axis=1)
        parts = [folded[:, at : at + columns] for at in range(half, folded.shape[1], columns)]
        grad_b = grad_b + jnp.concatenate(parts, axis=0)
    for at in range(6):
        fetch(at).wait()
    made[0][...], made[1][...], made[2][...] = adaptive_moment_step(a[...], grad_a, am[...], av[...])
    padding = jnp.zeros((left.shape[0] - rows, inner), F32)
    left[...] = jnp.concatenate([made[0][...], padding], axis=0).astype(BF16)
    next_b, first_b, second_b = adaptive_moment_step(b[...], grad_b, bm[...], bv[...])
    for array, result in zip((next_b, first_b, second_b), made[3:]):
        result[...] = pick(me, [array[j * rows : (j + 1) * rows] for j in range(replicas)])
    for at in range(6):
        keep(at).start()
    width = columns // replicas
    choices = [next_b[:, j * width : (j + 1) * width] for j in range(replicas)]
    sent[...] = pick(me, choices).astype(BF16)
    product = dot_nt(x, left)
    empty = jnp.zeros((product.shape[0], LANES - left.shape[0]), F32)
    out[...] = jnp.transpose(jnp.concatenate([product, empty], axis=1))[0:rows, :]
    for at in range(6):
        keep(at).wait()


def rollout_kernel(following, x, given, *rest):
    if following is None:
        (out,) = rest
    else:
        w, out, after, arrived = rest
    me = lax.axis_index("tensor")
    width = out.shape[1]

    if following is not None:
        start = pl.multiple_of(lax.bitwise_xor(me, following) * width, width)
        next_one = pltpu.make_async_copy(w.at[:, pl.ds(start, width)], after, arrived)
        next_one.start()
    out[...] = dot(x[...], given[...]).astype(out.dtype)
    if following is not None:
        next_one.wait()


def gather_kernel(bit, mine, arrived, out):
    later = lax.bitwise_and(lax.shift_right_logical(lax.axis_index("dp"), bit), 1) == 1
    first = jnp.where(later, arrived[...], mine[...])
    out[...] = jnp.concatenate([first, jnp.where(later, mine[...], arrived[...])], axis=0)


def join_kernel(*refs):
    total = refs[0][...].astype(F32)
    for leaf in refs[1:-1]:
        total = total + leaf[...].astype(F32)
    refs[-1][...] = total.astype(refs[-1].dtype)


def finish_kernel(rank, factor, mine, arrived, *rest):
    leaves, (out, made, kept) = rest[:-3], rest[-3:]
    high, low = split_bf16(mine[...] + arrived[...])
    empty = jnp.zeros((LANES - 2 * rank, high.shape[1]), F32)
    wide = jnp.concatenate([high.astype(F32), low.astype(F32), empty], axis=0)
    tall = jnp.transpose(wide).astype(BF16)
    empty = jnp.zeros((LANES - 2 * rank, factor.shape[1]), BF16)
    total = adapter_scale * dot(tall, jnp.concatenate([factor[...], factor[...], empty], axis=0))
    for leaf in leaves:
        total = total + leaf[...].astype(F32)
    made[...] = total.astype(BF16)
    copy = pltpu.make_async_copy(made, out, kept)
    copy.start()
    copy.wait()


def shards(
    hidden,
    cotangent,
    prompt_group_index,
    answer_token_mask,
    token_reward_order,
    source_lowdim_matrix,
    running_mean_source_matrix,
    running_variance_source_matrix,
    target_lowdim_matrix,
    running_mean_target_matrix,
    running_variance_target_matrix,
    frozen_down_weight,
    sampled_token_input,
):
    replicas, peers = lax.axis_size("dp"), lax.axis_size("tensor")
    me_dp = lax.axis_index("dp")
    x, w = sampled_token_input, frozen_down_weight
    tokens, inner = hidden.shape
    columns = cotangent.shape[1]
    rank = source_lowdim_matrix.shape[0]
    rows = rank // replicas
    groups = tokens * replicas // 8
    rollout = x.shape[0]
    own_width = w.shape[1] // peers
    deep = tile_of(inner, 1664)

    def xor(array, k, axis="tensor"):
        return lax.ppermute(array, axis, [(i, i ^ k) for i in range(lax.axis_size(axis))])

    def add(arrays, after=()):
        (total,) = call(
            join_kernel, "join", arrays, [], [shape(arrays[0].shape, arrays[-1].dtype)], [], [], 0, 8, after
        )
        return total

    chips = peers // 2
    todo = [(m, other) for m in range(chips - 1, -1, -1) for other in (1, 0)]
    crossed, arrived, own, waiting = {}, {}, {}, []

    def form(eighths, after):
        nonlocal handed
        for _ in range(eighths * len(todo_all) // 8):
            m, other = todo.pop(0)
            following = 2 * todo[0][0] + todo[0][1] if todo else None
            result = shape((rollout, own_width), BF16 if other else F32)
            block = shape((inner, own_width), BF16)
            result, *handed = call(
                functools.partial(rollout_kernel, following),
                "rollout%d%d" % (m, other),
                [x_held, handed],
                [w] if following is not None else [],
                [result] + ([block] if following is not None else []),
                [],
                [pltpu.SemaphoreType.DMA(())] if following is not None else [],
                2 * rollout * inner * own_width,
                20,
                after,
            )
            handed = handed[0] if handed else None
            if other:
                crossed[m] = xor(result, 1)
            else:
                own[m] = result
                waiting.append(m)
            after = [result]
        return after

    def leaves_of(m):
        bits = [1 << at for at in range(chips.bit_length() - 1)]
        lower = [bit for bit in bits if not m or bit < m & -m]
        return [own[m], crossed[m], *[arrived[m | bit] for bit in lower]]

    def send_on(after):
        while waiting:
            m = waiting.pop(0)
            total = add(leaves_of(m), after)
            arrived[m] = xor(total, 2 * (m & -m))
            after = [total]
        return after

    todo_all = list(todo)

    tok = [
        array.reshape(1, tokens) for array in (prompt_group_index, answer_token_mask, token_reward_order)
    ]
    packed, stats, tok_held, hidden_held, cot_held, x_held, handed = call(
        functools.partial(project_kernel, 2 * todo[0][0] + todo[0][1]),
        "project",
        [],
        [*tok, hidden, source_lowdim_matrix, cotangent, target_lowdim_matrix, x, w],
        [
            shape((tokens // 2, LANES), F32),
            shape((8, groups), F32),
            shape((8, tokens), jnp.int32),
            shape(hidden.shape, BF16),
            shape(cotangent.shape, BF16),
            shape(x.shape, BF16),
            shape((inner, own_width), BF16),
        ],
        [],
        [pltpu.VMEM((1, tokens), jnp.int32)] * 3
        + [
            pltpu.VMEM((rank, inner), F32),
            pltpu.VMEM((rank, columns), F32),
            pltpu.SemaphoreType.DMA((inner // deep + 8,)),
        ],
        2 * tokens * (inner + columns) * 256,
        38.6,
    )
    all_stats = [stats] + [xor(stats, k, "dp") for k in range(1, replicas)]
    tensor_bits = [1 << at for at in range(peers.bit_length() - 1)]
    received = xor(packed, tensor_bits[0])
    after = form(1, [packed])
    for bit in tensor_bits[1:]:
        packed = add([packed, received], after)
        received = xor(packed, bit)
        after = form(1, [packed]) if bit in (2, 4) else [packed]
    after = send_on(after)

    own_a, own_b, *sent = call(
        functools.partial(gradient_kernel, replicas, rank),
        "gradient",
        [tok_held, packed, received, hidden_held, cot_held, *all_stats],
        [],
        [shape((rows, inner), F32), shape((rank, columns), F32)]
        + [shape((2 * rows, inner // 2 + columns * replicas // 2), BF16)] * (replicas - 1),
        [],
        [pltpu.VMEM((tokens, LANES), F32), pltpu.VMEM((rank, inner), F32)],
        2 * tokens * (inner + columns) * 256,
        16,
        after,
    )
    received = [xor(array, k + 1, "dp") for k, array in enumerate(sent)]
    after = send_on(form(1, [own_a]))

    left = [source_lowdim_matrix, running_mean_source_matrix, running_variance_source_matrix]
    right = [target_lowdim_matrix, running_mean_target_matrix, running_variance_target_matrix]
    if rows % 8:
        left = [lax.dynamic_slice_in_dim(array, me_dp * rows, rows, 0) for array in left]
    own_left, own_right = shape((rows, inner), F32), shape((rows, columns), F32)
    sent_b, product, *updated = call(
        functools.partial(update_kernel, replicas),
        "update",
        [own_a, own_b, x_held, *received],
        [*left, *right],
        [shape((rank, columns // replicas), BF16), shape((rows, rollout), F32)],
        [own_left] * 3 + [own_right] * 3,
        [pltpu.VMEM((rows, inner), F32)] * 3
        + [pltpu.VMEM((rank, columns), F32)] * 3
        + [pltpu.VMEM((rows, inner), F32)] * 3
        + [pltpu.VMEM((rows, columns), F32)] * 3
        + [pltpu.SemaphoreType.DMA((6,)), pltpu.VMEM((16, inner), BF16)],
        2 * rollout * inner * 256,
        24,
        after,
    )
    pairs = [(dp * peers + at, at * replicas + dp) for dp in range(replicas) for at in range(peers)]
    factor = lax.ppermute(sent_b, ("dp", "tensor"), pairs)
    after = [product]
    for at in range(replicas.bit_length() - 1):
        received = xor(product, 1 << at, "dp")
        if at < 2:
            after = form(1, after)
        if at == replicas.bit_length() - 2:
            after = after + [factor]
        both = shape((2 * product.shape[0], rollout), F32)
        (product,) = call(
            functools.partial(gather_kernel, at), "gather", [product, received], [], [both], [], [], 0, 8, after
        )
        after = [product]
    for at, bit in enumerate(tensor_bits):
        received = xor(product, bit)
        if at < 2 and todo:
            after = form(1 if at == 0 else len(todo) * 8 // len(todo_all), after)
        if at < len(tensor_bits) - 1:
            product = add([product, received], after)
            after = [product]
        if at == 0:
            after = send_on(after)
    waiting.remove(0)
    send_on(after)

    (result,) = call(
        functools.partial(finish_kernel, rank),
        "finish",
        [factor, product, received, *leaves_of(0)],
        [],
        [],
        [shape((rollout, own_width), BF16)],
        [pltpu.VMEM((rollout, own_width), BF16), pltpu.SemaphoreType.DMA(())],
        2 * rollout * own_width * 256,
        16,
    )
    return (result, *updated)


def solution(mesh):
    placed = (
        P("dp", "tensor"),
        P("dp", "tensor"),
        P("dp"),
        P("dp"),
        P("dp"),
        P(None, "tensor"),
        P(None, "tensor"),
        P(None, "tensor"),
        P(None, "tensor"),
        P(None, "tensor"),
        P(None, "tensor"),
        P("tensor", "dp"),
        P(None, "tensor"),
    )
    return jax.shard_map(
        shards,
        mesh=mesh,
        in_specs=placed,
        out_specs=(P(None, ("dp", "tensor")), *[P("dp", "tensor")] * 6),
        check_vma=False,
    )
```

```python
import functools

import jax
import jax.numpy as jnp
from jax import lax
from jax.experimental import pallas as pl
from jax.experimental.pallas import tpu as pltpu
from jax.sharding import PartitionSpec as P

adapter_scale = 2.0
bias_one = 1.0 - 0.9**10
bias_two = 1.0 - 0.999**10

F32 = jnp.float32
BF16 = jnp.bfloat16
LANES = 128
MIB = 1 << 20


def dot(a, b):
    return jnp.dot(a, b, preferred_element_type=F32)


def dot_nt(a, b):
    length = a.shape[1]
    cut = length // 512 * 256
    if cut < 512:
        return dot_nt_part(a, b, 0, length)
    return dot_nt_part(a, b, 0, cut) + dot_nt_part(a, b, cut, length)


def dot_nt_part(a, b, first, last):
    dims = (((1,), (1,)), ((), ()))
    return lax.dot_general(a[:, first:last], b[:, first:last], dims, preferred_element_type=F32)


def adaptive_moment_step(param, grad, first, second):
    first = 0.9 * first + 0.1 * grad
    second = 0.999 * second + 0.001 * grad * grad
    param = param - 0.004 * (first / bias_one) / (jnp.sqrt(second / bias_two) + 1e-08)
    return (param, first, second)


def tile_of(length, limit):
    units = length // LANES
    return LANES * max(u for u in range(1, limit // LANES + 1) if units % u == 0)


def split_bf16(value):
    high = value.astype(BF16)
    return high, (value - high.astype(F32)).astype(BF16)


def pick(index, choices):
    result = choices[0]
    for at in range(1, len(choices)):
        result = jnp.where(index == at, choices[at], result)
    return result


def shape(dims, kind):
    return jax.ShapeDtypeStruct(dims, kind)


ANY = pl.BlockSpec(memory_space=pl.ANY)
HBM = pl.BlockSpec(memory_space=pltpu.HBM)
VMEM = pl.BlockSpec(memory_space=pltpu.VMEM)


def call(kernel, name, held, far, outputs, far_outputs, scratch, flops, vmem, after=()):
    first = len(held) + len(far)
    moved = sum(a.size * a.dtype.itemsize for a in [*far, *far_outputs])

    def body(*refs):
        kernel(*refs[:first], *refs[first + len(after) :])

    return pl.pallas_call(
        body,
        name=name,
        out_shape=[*outputs, *far_outputs],
        in_specs=[VMEM] * len(held) + [HBM] * len(far) + [ANY] * len(after),
        out_specs=[VMEM] * len(outputs) + [HBM] * len(far_outputs),
        scratch_shapes=scratch,
        compiler_params=pltpu.CompilerParams(vmem_limit_bytes=int(vmem * MIB)),
        cost_estimate=pl.CostEstimate(flops=flops, bytes_accessed=moved, transcendentals=0),
    )(*held, *far, *after)


def in_turn(fetches, ahead=2):
    for fetch in fetches[:ahead]:
        fetch.start()
    done = []

    def arrive():
        fetches[len(done)].wait()
        done.append(True)
        if len(done) - 1 + ahead < len(fetches):
            fetches[len(done) - 1 + ahead].start()

    return arrive


def project_kernel(index, mask, order, far_hidden, far_a, far_cot, far_b, packed, stats, *rest):
    hidden, a, cot, b, arrived = rest
    rank = a.shape[0]
    inner = hidden.shape[1]
    chunks = arrived.shape[0] - 3
    width = inner // chunks
    pairs = [(far_a, a)]
    for at in range(chunks):
        columns = slice(at * width, (at + 1) * width)
        pairs.append((far_hidden.at[:, columns], hidden.at[:, columns]))
    pairs += [(far_cot, cot), (far_b, b)]
    fetches = [pltpu.make_async_copy(*pair, arrived.at[at]) for at, pair in enumerate(pairs)]
    arrive = in_turn(fetches, 3)
    arrive()
    left = a[...].astype(BF16)
    total = None
    for at in range(chunks):
        arrive()
        columns = slice(at * width, (at + 1) * width)
        product = dot_nt(hidden.at[:, columns], left[:, columns])
        total = product if total is None else total + product
    arrive()
    arrive()
    high, low = split_bf16(b[...])
    both = dot_nt(cot, jnp.concatenate([high, low], axis=0))
    both = jnp.concatenate([total, both[:, :rank] + both[:, rank:]], axis=1)
    half = both.shape[0] // 2
    packed[...] = jnp.concatenate([both[:half], both[half:]], axis=1)
    groups, tokens = stats.shape[1], index.shape[1]
    member = (lax.broadcasted_iota(jnp.int32, (groups, tokens), 0) == index[...]).astype(F32)
    row = lax.broadcasted_iota(jnp.int32, (8, tokens), 0)
    values = jnp.where(row == 0, mask[...], 0)
    values = jnp.where(row == 1, mask[...] * order[...], values)
    values = jnp.where(row == 2, mask[...] * order[...] * order[...], values)
    stats[...] = dot_nt(values.astype(F32).astype(BF16), member.astype(BF16))


def gradient_kernel(replicas, rank, all_index, all_mask, all_order, packed, arrived, hidden, cot, *rest):
    stats, (own_a, own_b, *sent) = rest[:replicas], rest[replicas:-2]
    column, grad = rest[-2:]
    rows = rank // replicas
    me = lax.axis_index("dp")
    tokens, inner = hidden.shape
    groups = stats[0].shape[1]
    half = inner // 2
    sums = stats[0][...]
    for other in stats[1:]:
        sums = sums + other[...]
    counts, firsts, squares = sums[0:1, :], sums[1:2, :], sums[2:3, :]
    safe = jnp.maximum(counts, 1.0)
    mean = firsts / safe
    spread = jnp.maximum(jnp.sqrt(jnp.maximum(squares / safe - mean * mean, 0.0)), 1.0)
    total = jnp.maximum(jnp.sum(counts, axis=1, keepdims=True), 1.0)

    row = lax.broadcasted_iota(jnp.int32, (LANES, tokens), 0)
    tall = jnp.where(row == 0, all_index[...], 0)
    tall = jnp.where(row == 1, all_mask[...], tall)
    tall = jnp.where(row == 2, all_order[...], tall)
    column[...] = jnp.transpose(tall.astype(F32))
    index, mask, order = column[:, 0:1], column[:, 1:2], column[:, 2:3]
    member = index == lax.broadcasted_iota(jnp.int32, (tokens, groups), 1).astype(F32)
    own_mean = jnp.sum(jnp.where(member, mean, 0.0), axis=1, keepdims=True)
    own_spread = jnp.sum(jnp.where(member, spread, 0.0), axis=1, keepdims=True)
    coefficient = -mask * (order - own_mean) / own_spread / total

    both = packed[...] + arrived[...]
    both = jnp.concatenate([both[:, : 2 * rank], both[:, 2 * rank : 4 * rank]], axis=0)
    both = both * coefficient
    back = both[:, rank:].astype(BF16).astype(F32)
    high, low = split_bf16(both[:, :rank])
    empty = jnp.zeros((tokens, LANES - 3 * rank), F32)
    tall = jnp.concatenate([back, high.astype(F32), low.astype(F32), empty], axis=1)
    wide = jnp.transpose(tall).astype(BF16)
    grad[...] = adapter_scale * dot(wide[0:rank, :], hidden[...])
    both = dot(wide[rank : 3 * rank, :], cot[...])
    whole = adapter_scale * (both[:rank] + both[rank:])
    pieces = [grad[j * rows : (j + 1) * rows, :] for j in range(replicas)]
    own_a[...] = pick(me, pieces)
    own_b[...] = whole
    folded = [whole[at : at + 2 * rows] for at in range(0, rank, 2 * rows)]
    folded = jnp.concatenate(folded, axis=1).astype(BF16)
    for k in range(1, replicas):
        piece = pick(lax.bitwise_xor(me, k), pieces)
        halves = jnp.concatenate([piece[:, :half], piece[:, half:]], axis=0)
        sent[k - 1][:, 0:half] = halves.astype(BF16)
        sent[k - 1][:, half:] = folded


def update_kernel(replicas, own_a, own_b, x, *rest):
    received, rest = rest[: replicas - 1], rest[replicas - 1 :]
    factors, (sent, out), results = rest[:6], rest[6:8], rest[8:14]
    (a, am, av, b, bm, bv), made, arrived, left = rest[14:20], rest[20:26], rest[26], rest[27]
    rows, inner = a.shape
    rank, columns = b.shape
    me = lax.axis_index("dp")

    def fetch(at):
        source = factors[at]
        if at < 3 and source.shape[0] != rows:
            source = source.at[pl.ds(pl.multiple_of(me * rows, rows), rows), :]
        return pltpu.make_async_copy(source, (a, am, av, b, bm, bv)[at], arrived.at[at])

    def keep(at):
        return pltpu.make_async_copy(made[at], results[at], arrived.at[at])

    for at in range(6):
        fetch(at).start()
    grad_a, grad_b = own_a[...], own_b[...]
    half = inner // 2
    for other in received:
        folded = other[...].astype(F32)
        grad_a = grad_a + jnp.concatenate([folded[:rows, :half], folded[rows:, :half]], axis=1)
        parts = [folded[:, at : at + columns] for at in range(half, folded.shape[1], columns)]
        grad_b = grad_b + jnp.concatenate(parts, axis=0)
    for at in range(6):
        fetch(at).wait()
    made[0][...], made[1][...], made[2][...] = adaptive_moment_step(a[...], grad_a, am[...], av[...])
    padding = jnp.zeros((left.shape[0] - rows, inner), F32)
    left[...] = jnp.concatenate([made[0][...], padding], axis=0).astype(BF16)
    next_b, first_b, second_b = adaptive_moment_step(b[...], grad_b, bm[...], bv[...])
    for array, result in zip((next_b, first_b, second_b), made[3:]):
        result[...] = pick(me, [array[j * rows : (j + 1) * rows] for j in range(replicas)])
    for at in range(6):
        keep(at).start()
    width = columns // replicas
    choices = [next_b[:, j * width : (j + 1) * width] for j in range(replicas)]
    sent[...] = pick(me, choices).astype(BF16)
    product = dot_nt(x, left)
    empty = jnp.zeros((product.shape[0], LANES - left.shape[0]), F32)
    out[...] = jnp.transpose(jnp.concatenate([product, empty], axis=1))[0:rows, :]
    for at in range(6):
        keep(at).wait()


def rollout_kernel(differs, following, first, x, *rest):
    if following is None:
        given, out = rest
    elif first:
        w, out, after, given, arrived = rest
    else:
        given, w, out, after, arrived = rest
    me = lax.axis_index("tensor")
    width = out.shape[1]
    parts = 4
    height = x.shape[1] // parts

    def fetch(differs, held, row):
        start = pl.multiple_of(lax.bitwise_xor(me, differs) * width, width)
        copies = []
        for at in range(parts):
            rows = slice(at * height, (at + 1) * height)
            source = w.at[rows, pl.ds(start, width)]
            copies.append(pltpu.make_async_copy(source, held.at[rows, :], arrived.at[row, at]))
        for copy in copies:
            copy.start()
        return copies

    if first:
        for copy in fetch(differs, given, 0):
            copy.wait()
    copies = [] if following is None else fetch(following, after, 1)
    out[...] = dot(x[...], given[...]).astype(out.dtype)
    for copy in copies:
        copy.wait()


def gather_kernel(bit, mine, arrived, out):
    later = lax.bitwise_and(lax.shift_right_logical(lax.axis_index("dp"), bit), 1) == 1
    first = jnp.where(later, arrived[...], mine[...])
    out[...] = jnp.concatenate([first, jnp.where(later, mine[...], arrived[...])], axis=0)


def join_kernel(*refs):
    total = refs[0][...].astype(F32)
    for leaf in refs[1:-1]:
        total = total + leaf[...].astype(F32)
    refs[-1][...] = total.astype(refs[-1].dtype)


def finish_kernel(rank, factor, mine, arrived, *rest):
    leaves, (out, made, kept) = rest[:-3], rest[-3:]
    high, low = split_bf16(mine[...] + arrived[...])
    empty = jnp.zeros((LANES - 2 * rank, high.shape[1]), F32)
    wide = jnp.concatenate([high.astype(F32), low.astype(F32), empty], axis=0)
    tall = jnp.transpose(wide).astype(BF16)
    empty = jnp.zeros((LANES - 2 * rank, factor.shape[1]), BF16)
    total = adapter_scale * dot(tall, jnp.concatenate([factor[...], factor[...], empty], axis=0))
    for leaf in leaves:
        total = total + leaf[...].astype(F32)
    made[...] = total.astype(BF16)
    copy = pltpu.make_async_copy(made, out, kept)
    copy.start()
    copy.wait()


def shards(
    hidden,
    cotangent,
    prompt_group_index,
    answer_token_mask,
    token_reward_order,
    source_lowdim_matrix,
    running_mean_source_matrix,
    running_variance_source_matrix,
    target_lowdim_matrix,
    running_mean_target_matrix,
    running_variance_target_matrix,
    frozen_down_weight,
    sampled_token_input,
):
    replicas, peers = lax.axis_size("dp"), lax.axis_size("tensor")
    me_dp = lax.axis_index("dp")
    x, w = sampled_token_input, frozen_down_weight
    tokens, inner = hidden.shape
    columns = cotangent.shape[1]
    rank = source_lowdim_matrix.shape[0]
    rows = rank // replicas
    groups = tokens * replicas // 8
    rollout = x.shape[0]
    own_width = w.shape[1] // peers
    deep = tile_of(inner, 1664)

    def xor(array, k, axis="tensor"):
        return lax.ppermute(array, axis, [(i, i ^ k) for i in range(lax.axis_size(axis))])

    def add(arrays, after=()):
        (total,) = call(
            join_kernel, "join", arrays, [], [shape(arrays[0].shape, arrays[-1].dtype)], [], [], 0, 8, after
        )
        return total

    chips = peers // 2
    todo = [(m, other) for m in range(chips - 1, -1, -1) for other in (1, 0)]
    crossed, arrived, own, waiting, handed = {}, {}, {}, [], None

    def form(eighths, after):
        nonlocal handed
        for _ in range(eighths * len(todo_all) // 8):
            m, other = todo.pop(0)
            following = 2 * todo[0][0] + todo[0][1] if todo else None
            first = handed is None
            outputs = [shape((rollout, own_width), BF16 if other else F32)]
            block = shape((inner, own_width), BF16)
            result, *handed = call(
                functools.partial(rollout_kernel, 2 * m + other, following, first),
                "rollout%d%d" % (m, other),
                [x] if first else [x, handed],
                [] if following is None else [w],
                outputs + ([] if following is None else [block]),
                [],
                ([pltpu.VMEM(block.shape, BF16)] if first else [])
                + ([] if following is None else [pltpu.SemaphoreType.DMA((2, 4))]),
                2 * rollout * inner * own_width,
                12,
                after,
            )
            handed = handed[0] if handed else None
            if other:
                crossed[m] = xor(result, 1)
            else:
                own[m] = result
                waiting.append(m)
            after = [result]
        return after

    def leaves_of(m):
        bits = [1 << at for at in range(chips.bit_length() - 1)]
        lower = [bit for bit in bits if not m or bit < m & -m]
        return [own[m], crossed[m], *[arrived[m | bit] for bit in lower]]

    def send_on(after):
        while waiting:
            m = waiting.pop(0)
            total = add(leaves_of(m), after)
            arrived[m] = xor(total, 2 * (m & -m))
            after = [total]
        return after

    todo_all = list(todo)

    tok = [
        array.reshape(1, tokens) for array in (prompt_group_index, answer_token_mask, token_reward_order)
    ]
    packed, stats = call(
        project_kernel,
        "project",
        tok,
        [hidden, source_lowdim_matrix, cotangent, target_lowdim_matrix],
        [shape((tokens // 2, LANES), F32), shape((8, groups), F32)],
        [],
        [
            pltpu.VMEM((tokens, inner), BF16),
            pltpu.VMEM((rank, inner), F32),
            pltpu.VMEM((tokens, columns), BF16),
            pltpu.VMEM((rank, columns), F32),
            pltpu.SemaphoreType.DMA((inner // deep + 3,)),
        ],
        2 * tokens * (inner + columns) * 256,
        54,
    )
    all_stats = [stats] + [xor(stats, k, "dp") for k in range(1, replicas)]
    tensor_bits = [1 << at for at in range(peers.bit_length() - 1)]
    received = xor(packed, tensor_bits[0])
    after = form(1, [packed])
    for bit in tensor_bits[1:]:
        packed = add([packed, received], after)
        received = xor(packed, bit)
        after = form(1, [packed]) if bit in (2, 4) else [packed]
    after = send_on(after)

    own_a, own_b, *sent = call(
        functools.partial(gradient_kernel, replicas, rank),
        "gradient",
        [*tok, packed, received, hidden, cotangent, *all_stats],
        [],
        [shape((rows, inner), F32), shape((rank, columns), F32)]
        + [shape((2 * rows, inner // 2 + columns * replicas // 2), BF16)] * (replicas - 1),
        [],
        [pltpu.VMEM((tokens, LANES), F32), pltpu.VMEM((rank, inner), F32)],
        2 * tokens * (inner + columns) * 256,
        16,
        after,
    )
    received = [xor(array, k + 1, "dp") for k, array in enumerate(sent)]
    after = send_on(form(1, [own_a]))

    left = [source_lowdim_matrix, running_mean_source_matrix, running_variance_source_matrix]
    right = [target_lowdim_matrix, running_mean_target_matrix, running_variance_target_matrix]
    if rows % 8:
        left = [lax.dynamic_slice_in_dim(array, me_dp * rows, rows, 0) for array in left]
    own_left, own_right = shape((rows, inner), F32), shape((rows, columns), F32)
    sent_b, product, *updated = call(
        functools.partial(update_kernel, replicas),
        "update",
        [own_a, own_b, x, *received],
        [*left, *right],
        [shape((rank, columns // replicas), BF16), shape((rows, rollout), F32)],
        [own_left] * 3 + [own_right] * 3,
        [pltpu.VMEM((rows, inner), F32)] * 3
        + [pltpu.VMEM((rank, columns), F32)] * 3
        + [pltpu.VMEM((rows, inner), F32)] * 3
        + [pltpu.VMEM((rows, columns), F32)] * 3
        + [pltpu.SemaphoreType.DMA((6,)), pltpu.VMEM((16, inner), BF16)],
        2 * rollout * inner * 256,
        24,
        after,
    )
    pairs = [(dp * peers + at, at * replicas + dp) for dp in range(replicas) for at in range(peers)]
    factor = lax.ppermute(sent_b, ("dp", "tensor"), pairs)
    after = [product]
    for at in range(replicas.bit_length() - 1):
        received = xor(product, 1 << at, "dp")
        if at < 2:
            after = form(1, after)
            if at:
                after = send_on(after)
        if at == replicas.bit_length() - 2:
            after = after + [factor]
        both = shape((2 * product.shape[0], rollout), F32)
        (product,) = call(
            functools.partial(gather_kernel, at), "gather", [product, received], [], [both], [], [], 0, 8, after
        )
        after = [product]
    for at, bit in enumerate(tensor_bits):
        received = xor(product, bit)
        if at < 2 and todo:
            after = form(1 if at == 0 else len(todo) * 8 // len(todo_all), after)
        if at < len(tensor_bits) - 1:
            product = add([product, received], after)
            after = [product]
    waiting.remove(0)
    send_on(after)

    (result,) = call(
        functools.partial(finish_kernel, rank),
        "finish",
        [factor, product, received, *leaves_of(0)],
        [],
        [],
        [shape((rollout, own_width), BF16)],
        [pltpu.VMEM((rollout, own_width), BF16), pltpu.SemaphoreType.DMA(())],
        2 * rollout * own_width * 256,
        16,
    )
    return (result, *updated)


def solution(mesh):
    placed = (
        P("dp", "tensor"),
        P("dp", "tensor"),
        P("dp"),
        P("dp"),
        P("dp"),
        P(None, "tensor"),
        P(None, "tensor"),
        P(None, "tensor"),
        P(None, "tensor"),
        P(None, "tensor"),
        P(None, "tensor"),
        P("tensor", "dp"),
        P(None, "tensor"),
    )
    return jax.shard_map(
        shards,
        mesh=mesh,
        in_specs=placed,
        out_specs=(P(None, ("dp", "tensor")), *[P("dp", "tensor")] * 6),
        check_vma=False,
    )
```

```python
import functools

import jax
import jax.numpy as jnp
from jax import lax
from jax.experimental import pallas as pl
from jax.experimental.pallas import tpu as pltpu
from jax.sharding import PartitionSpec as P

adapter_scale = 2.0
bias_one = 1.0 - 0.9**10
bias_two = 1.0 - 0.999**10

F32 = jnp.float32
BF16 = jnp.bfloat16
LANES = 128
MIB = 1 << 20


def dot(a, b):
    return jnp.dot(a, b, preferred_element_type=F32)


def dot_nt(a, b):
    length = a.shape[1]
    cut = length // 512 * 256
    if cut < 512:
        return dot_nt_part(a, b, 0, length)
    return dot_nt_part(a, b, 0, cut) + dot_nt_part(a, b, cut, length)


def dot_nt_part(a, b, first, last):
    dims = (((1,), (1,)), ((), ()))
    return lax.dot_general(a[:, first:last], b[:, first:last], dims, preferred_element_type=F32)


def adaptive_moment_step(param, grad, first, second):
    first = 0.9 * first + 0.1 * grad
    second = 0.999 * second + 0.001 * grad * grad
    param = param - 0.004 * (first / bias_one) / (jnp.sqrt(second / bias_two) + 1e-08)
    return (param, first, second)


def tile_of(length, limit):
    units = length // LANES
    return LANES * max(u for u in range(1, limit // LANES + 1) if units % u == 0)


def split_bf16(value):
    high = value.astype(BF16)
    return high, (value - high.astype(F32)).astype(BF16)


def pick(index, choices):
    result = choices[0]
    for at in range(1, len(choices)):
        result = jnp.where(index == at, choices[at], result)
    return result


def shape(dims, kind):
    return jax.ShapeDtypeStruct(dims, kind)


ANY = pl.BlockSpec(memory_space=pl.ANY)
HBM = pl.BlockSpec(memory_space=pltpu.HBM)
VMEM = pl.BlockSpec(memory_space=pltpu.VMEM)


def call(kernel, name, held, far, outputs, far_outputs, scratch, flops, vmem, after=()):
    first = len(held) + len(far)
    moved = sum(a.size * a.dtype.itemsize for a in [*far, *far_outputs])

    def body(*refs):
        kernel(*refs[:first], *refs[first + len(after) :])

    return pl.pallas_call(
        body,
        name=name,
        out_shape=[*outputs, *far_outputs],
        in_specs=[VMEM] * len(held) + [HBM] * len(far) + [ANY] * len(after),
        out_specs=[VMEM] * len(outputs) + [HBM] * len(far_outputs),
        scratch_shapes=scratch,
        compiler_params=pltpu.CompilerParams(vmem_limit_bytes=int(vmem * MIB)),
        cost_estimate=pl.CostEstimate(flops=flops, bytes_accessed=moved, transcendentals=0),
    )(*held, *far, *after)


def in_turn(fetches, ahead=2):
    for fetch in fetches[:ahead]:
        fetch.start()
    done = []

    def arrive():
        fetches[len(done)].wait()
        done.append(True)
        if len(done) - 1 + ahead < len(fetches):
            fetches[len(done) - 1 + ahead].start()

    return arrive


def project_kernel(index, mask, order, far_hidden, far_a, far_cot, far_b, packed, stats, *rest):
    hidden, a, cot, b, arrived = rest
    rank = a.shape[0]
    inner = hidden.shape[1]
    chunks = arrived.shape[0] - 3
    width = inner // chunks
    pairs = [(far_a, a)]
    for at in range(chunks):
        columns = slice(at * width, (at + 1) * width)
        pairs.append((far_hidden.at[:, columns], hidden.at[:, columns]))
    pairs += [(far_cot, cot), (far_b, b)]
    fetches = [pltpu.make_async_copy(*pair, arrived.at[at]) for at, pair in enumerate(pairs)]
    arrive = in_turn(fetches, 3)
    arrive()
    left = a[...].astype(BF16)
    total = None
    for at in range(chunks):
        arrive()
        columns = slice(at * width, (at + 1) * width)
        product = dot_nt(hidden.at[:, columns], left[:, columns])
        total = product if total is None else total + product
    arrive()
    arrive()
    high, low = split_bf16(b[...])
    both = dot_nt(cot, jnp.concatenate([high, low], axis=0))
    both = jnp.concatenate([total, both[:, :rank] + both[:, rank:]], axis=1)
    half = both.shape[0] // 2
    packed[...] = jnp.concatenate([both[:half], both[half:]], axis=1)
    groups, tokens = stats.shape[1], index.shape[1]
    member = (lax.broadcasted_iota(jnp.int32, (groups, tokens), 0) == index[...]).astype(F32)
    row = lax.broadcasted_iota(jnp.int32, (8, tokens), 0)
    values = jnp.where(row == 0, mask[...], 0)
    values = jnp.where(row == 1, mask[...] * order[...], values)
    values = jnp.where(row == 2, mask[...] * order[...] * order[...], values)
    stats[...] = dot_nt(values.astype(F32).astype(BF16), member.astype(BF16))


def gradient_kernel(replicas, rank, all_index, all_mask, all_order, packed, arrived, hidden, cot, *rest):
    stats, (own_a, own_b, *sent) = rest[:replicas], rest[replicas:-2]
    column, grad = rest[-2:]
    rows = rank // replicas
    me = lax.axis_index("dp")
    tokens, inner = hidden.shape
    groups = stats[0].shape[1]
    half = inner // 2
    sums = stats[0][...]
    for other in stats[1:]:
        sums = sums + other[...]
    counts, firsts, squares = sums[0:1, :], sums[1:2, :], sums[2:3, :]
    safe = jnp.maximum(counts, 1.0)
    mean = firsts / safe
    spread = jnp.maximum(jnp.sqrt(jnp.maximum(squares / safe - mean * mean, 0.0)), 1.0)
    total = jnp.maximum(jnp.sum(counts, axis=1, keepdims=True), 1.0)

    row = lax.broadcasted_iota(jnp.int32, (LANES, tokens), 0)
    tall = jnp.where(row == 0, all_index[...], 0)
    tall = jnp.where(row == 1, all_mask[...], tall)
    tall = jnp.where(row == 2, all_order[...], tall)
    column[...] = jnp.transpose(tall.astype(F32))
    index, mask, order = column[:, 0:1], column[:, 1:2], column[:, 2:3]
    member = index == lax.broadcasted_iota(jnp.int32, (tokens, groups), 1).astype(F32)
    own_mean = jnp.sum(jnp.where(member, mean, 0.0), axis=1, keepdims=True)
    own_spread = jnp.sum(jnp.where(member, spread, 0.0), axis=1, keepdims=True)
    coefficient = -mask * (order - own_mean) / own_spread / total

    both = packed[...] + arrived[...]
    both = jnp.concatenate([both[:, : 2 * rank], both[:, 2 * rank : 4 * rank]], axis=0)
    both = both * coefficient
    back = both[:, rank:].astype(BF16).astype(F32)
    high, low = split_bf16(both[:, :rank])
    empty = jnp.zeros((tokens, LANES - 3 * rank), F32)
    tall = jnp.concatenate([back, high.astype(F32), low.astype(F32), empty], axis=1)
    wide = jnp.transpose(tall).astype(BF16)
    grad[...] = adapter_scale * dot(wide[0:rank, :], hidden[...])
    both = dot(wide[rank : 3 * rank, :], cot[...])
    whole = adapter_scale * (both[:rank] + both[rank:])
    pieces = [grad[j * rows : (j + 1) * rows, :] for j in range(replicas)]
    own_a[...] = pick(me, pieces)
    own_b[...] = whole
    folded = [whole[at : at + 2 * rows] for at in range(0, rank, 2 * rows)]
    folded = jnp.concatenate(folded, axis=1).astype(BF16)
    for k in range(1, replicas):
        piece = pick(lax.bitwise_xor(me, k), pieces)
        halves = jnp.concatenate([piece[:, :half], piece[:, half:]], axis=0)
        sent[k - 1][:, 0:half] = halves.astype(BF16)
        sent[k - 1][:, half:] = folded


def update_kernel(replicas, own_a, own_b, x, *rest):
    received, rest = rest[: replicas - 1], rest[replicas - 1 :]
    factors, (sent, out), results = rest[:6], rest[6:8], rest[8:14]
    (a, am, av, b, bm, bv), made, arrived, left = rest[14:20], rest[20:26], rest[26], rest[27]
    rows, inner = a.shape
    rank, columns = b.shape
    me = lax.axis_index("dp")

    def fetch(at):
        source = factors[at]
        if at < 3 and source.shape[0] != rows:
            source = source.at[pl.ds(pl.multiple_of(me * rows, rows), rows), :]
        return pltpu.make_async_copy(source, (a, am, av, b, bm, bv)[at], arrived.at[at])

    def keep(at):
        return pltpu.make_async_copy(made[at], results[at], arrived.at[at])

    for at in range(6):
        fetch(at).start()
    grad_a, grad_b = own_a[...], own_b[...]
    half = inner // 2
    for other in received:
        folded = other[...].astype(F32)
        grad_a = grad_a + jnp.concatenate([folded[:rows, :half], folded[rows:, :half]], axis=1)
        parts = [folded[:, at : at + columns] for at in range(half, folded.shape[1], columns)]
        grad_b = grad_b + jnp.concatenate(parts, axis=0)
    for at in range(6):
        fetch(at).wait()
    made[0][...], made[1][...], made[2][...] = adaptive_moment_step(a[...], grad_a, am[...], av[...])
    padding = jnp.zeros((left.shape[0] - rows, inner), F32)
    left[...] = jnp.concatenate([made[0][...], padding], axis=0).astype(BF16)
    next_b, first_b, second_b = adaptive_moment_step(b[...], grad_b, bm[...], bv[...])
    for array, result in zip((next_b, first_b, second_b), made[3:]):
        result[...] = pick(me, [array[j * rows : (j + 1) * rows] for j in range(replicas)])
    for at in range(6):
        keep(at).start()
    width = columns // replicas
    choices = [next_b[:, j * width : (j + 1) * width] for j in range(replicas)]
    sent[...] = pick(me, choices).astype(BF16)
    product = dot_nt(x, left)
    empty = jnp.zeros((product.shape[0], LANES - left.shape[0]), F32)
    out[...] = jnp.transpose(jnp.concatenate([product, empty], axis=1))[0:rows, :]
    for at in range(6):
        keep(at).wait()


def rollout_kernel(differs, following, first, x, *rest):
    if following is None:
        given, out = rest
    elif first:
        w, out, after, given, arrived = rest
    else:
        given, w, out, after, arrived = rest
    me = lax.axis_index("tensor")
    width = out.shape[1]

    def fetch(differs, held, at):
        start = pl.multiple_of(lax.bitwise_xor(me, differs) * width, width)
        return pltpu.make_async_copy(w.at[:, pl.ds(start, width)], held, arrived.at[at])

    if first:
        own = fetch(differs, given, 0)
        own.start()
        own.wait()
    if following is not None:
        fetch(following, after, 1).start()

    @pl.when(me >= 0)
    def _():
        out[...] = dot(x[...], given[...]).astype(out.dtype)

    if following is not None:
        fetch(following, after, 1).wait()


def gather_kernel(bit, mine, arrived, out):
    later = lax.bitwise_and(lax.shift_right_logical(lax.axis_index("dp"), bit), 1) == 1
    first = jnp.where(later, arrived[...], mine[...])
    out[...] = jnp.concatenate([first, jnp.where(later, mine[...], arrived[...])], axis=0)


def join_kernel(*refs):
    total = refs[0][...].astype(F32)
    for leaf in refs[1:-1]:
        total = total + leaf[...].astype(F32)
    refs[-1][...] = total.astype(refs[-1].dtype)


def finish_kernel(rank, factor, mine, arrived, *rest):
    leaves, (out, made, kept) = rest[:-3], rest[-3:]
    high, low = split_bf16(mine[...] + arrived[...])
    empty = jnp.zeros((LANES - 2 * rank, high.shape[1]), F32)
    wide = jnp.concatenate([high.astype(F32), low.astype(F32), empty], axis=0)
    tall = jnp.transpose(wide).astype(BF16)
    empty = jnp.zeros((LANES - 2 * rank, factor.shape[1]), BF16)
    total = adapter_scale * dot(tall, jnp.concatenate([factor[...], factor[...], empty], axis=0))
    for leaf in leaves:
        total = total + leaf[...].astype(F32)
    made[...] = total.astype(BF16)
    copy = pltpu.make_async_copy(made, out, kept)
    copy.start()
    copy.wait()


def shards(
    hidden,
    cotangent,
    prompt_group_index,
    answer_token_mask,
    token_reward_order,
    source_lowdim_matrix,
    running_mean_source_matrix,
    running_variance_source_matrix,
    target_lowdim_matrix,
    running_mean_target_matrix,
    running_variance_target_matrix,
    frozen_down_weight,
    sampled_token_input,
):
    replicas, peers = lax.axis_size("dp"), lax.axis_size("tensor")
    me_dp = lax.axis_index("dp")
    x, w = sampled_token_input, frozen_down_weight
    tokens, inner = hidden.shape
    columns = cotangent.shape[1]
    rank = source_lowdim_matrix.shape[0]
    rows = rank // replicas
    groups = tokens * replicas // 8
    rollout = x.shape[0]
    own_width = w.shape[1] // peers
    deep = tile_of(inner, 1664)

    def xor(array, k, axis="tensor"):
        return lax.ppermute(array, axis, [(i, i ^ k) for i in range(lax.axis_size(axis))])

    def add(arrays, after=()):
        (total,) = call(
            join_kernel, "join", arrays, [], [shape(arrays[0].shape, arrays[-1].dtype)], [], [], 0, 8, after
        )
        return total

    chips = peers // 2
    todo = [(m, other) for m in range(chips - 1, -1, -1) for other in (1, 0)]
    crossed, arrived, own, waiting, handed = {}, {}, {}, [], None

    def form(eighths, after):
        nonlocal handed
        for _ in range(eighths * len(todo_all) // 8):
            m, other = todo.pop(0)
            following = 2 * todo[0][0] + todo[0][1] if todo else None
            first = handed is None
            outputs = [shape((rollout, own_width), BF16 if other else F32)]
            block = shape((inner, own_width), BF16)
            result, *handed = call(
                functools.partial(rollout_kernel, 2 * m + other, following, first),
                "rollout%d%d" % (m, other),
                [x] if first else [x, handed],
                [] if following is None else [w],
                outputs + ([] if following is None else [block]),
                [],
                ([pltpu.VMEM(block.shape, BF16)] if first else [])
                + ([] if following is None else [pltpu.SemaphoreType.DMA((2,))]),
                2 * rollout * inner * own_width,
                12,
                after,
            )
            handed = handed[0] if handed else None
            if other:
                crossed[m] = xor(result, 1)
            else:
                own[m] = result
                waiting.append(m)
            after = [result]
        return after

    def leaves_of(m):
        bits = [1 << at for at in range(chips.bit_length() - 1)]
        lower = [bit for bit in bits if not m or bit < m & -m]
        return [own[m], crossed[m], *[arrived[m | bit] for bit in lower]]

    def send_on(after):
        while waiting:
            m = waiting.pop(0)
            total = add(leaves_of(m), after)
            arrived[m] = xor(total, 2 * (m & -m))
            after = [total]
        return after

    todo_all = list(todo)

    tok = [
        array.reshape(1, tokens) for array in (prompt_group_index, answer_token_mask, token_reward_order)
    ]
    packed, stats = call(
        project_kernel,
        "project",
        tok,
        [hidden, source_lowdim_matrix, cotangent, target_lowdim_matrix],
        [shape((tokens // 2, LANES), F32), shape((8, groups), F32)],
        [],
        [
            pltpu.VMEM((tokens, inner), BF16),
            pltpu.VMEM((rank, inner), F32),
            pltpu.VMEM((tokens, columns), BF16),
            pltpu.VMEM((rank, columns), F32),
            pltpu.SemaphoreType.DMA((inner // deep + 3,)),
        ],
        2 * tokens * (inner + columns) * 256,
        54,
    )
    all_stats = [stats] + [xor(stats, k, "dp") for k in range(1, replicas)]
    tensor_bits = [1 << at for at in range(peers.bit_length() - 1)]
    received = xor(packed, tensor_bits[0])
    after = form(1, [packed])
    for bit in tensor_bits[1:]:
        packed = add([packed, received], after)
        received = xor(packed, bit)
        after = form(1, [packed]) if bit in (2, 4) else [packed]
    after = send_on(after)

    own_a, own_b, *sent = call(
        functools.partial(gradient_kernel, replicas, rank),
        "gradient",
        [*tok, packed, received, hidden, cotangent, *all_stats],
        [],
        [shape((rows, inner), F32), shape((rank, columns), F32)]
        + [shape((2 * rows, inner // 2 + columns * replicas // 2), BF16)] * (replicas - 1),
        [],
        [pltpu.VMEM((tokens, LANES), F32), pltpu.VMEM((rank, inner), F32)],
        2 * tokens * (inner + columns) * 256,
        16,
        after,
    )
    received = [xor(array, k + 1, "dp") for k, array in enumerate(sent)]
    after = send_on(form(1, [own_a]))

    left = [source_lowdim_matrix, running_mean_source_matrix, running_variance_source_matrix]
    right = [target_lowdim_matrix, running_mean_target_matrix, running_variance_target_matrix]
    if rows % 8:
        left = [lax.dynamic_slice_in_dim(array, me_dp * rows, rows, 0) for array in left]
    own_left, own_right = shape((rows, inner), F32), shape((rows, columns), F32)
    sent_b, product, *updated = call(
        functools.partial(update_kernel, replicas),
        "update",
        [own_a, own_b, x, *received],
        [*left, *right],
        [shape((rank, columns // replicas), BF16), shape((rows, rollout), F32)],
        [own_left] * 3 + [own_right] * 3,
        [pltpu.VMEM((rows, inner), F32)] * 3
        + [pltpu.VMEM((rank, columns), F32)] * 3
        + [pltpu.VMEM((rows, inner), F32)] * 3
        + [pltpu.VMEM((rows, columns), F32)] * 3
        + [pltpu.SemaphoreType.DMA((6,)), pltpu.VMEM((16, inner), BF16)],
        2 * rollout * inner * 256,
        24,
        after,
    )
    pairs = [(dp * peers + at, at * replicas + dp) for dp in range(replicas) for at in range(peers)]
    factor = lax.ppermute(sent_b, ("dp", "tensor"), pairs)
    after = [product]
    for at in range(replicas.bit_length() - 1):
        received = xor(product, 1 << at, "dp")
        if at < 2:
            after = form(1, after)
        if at == replicas.bit_length() - 2:
            after = after + [factor]
        both = shape((2 * product.shape[0], rollout), F32)
        (product,) = call(
            functools.partial(gather_kernel, at), "gather", [product, received], [], [both], [], [], 0, 8, after
        )
        after = [product]
    for at, bit in enumerate(tensor_bits):
        received = xor(product, bit)
        if at < 2 and todo:
            after = form(1 if at == 0 else len(todo) * 8 // len(todo_all), after)
        if at < len(tensor_bits) - 1:
            product = add([product, received], after)
            after = [product]
        if at == 0:
            after = send_on(after)
    waiting.remove(0)
    send_on(after)

    (result,) = call(
        functools.partial(finish_kernel, rank),
        "finish",
        [factor, product, received, *leaves_of(0)],
        [],
        [],
        [shape((rollout, own_width), BF16)],
        [pltpu.VMEM((rollout, own_width), BF16), pltpu.SemaphoreType.DMA(())],
        2 * rollout * own_width * 256,
        16,
    )
    return (result, *updated)


def solution(mesh):
    placed = (
        P("dp", "tensor"),
        P("dp", "tensor"),
        P("dp"),
        P("dp"),
        P("dp"),
        P(None, "tensor"),
        P(None, "tensor"),
        P(None, "tensor"),
        P(None, "tensor"),
        P(None, "tensor"),
        P(None, "tensor"),
        P("tensor", "dp"),
        P(None, "tensor"),
    )
    return jax.shard_map(
        shards,
        mesh=mesh,
        in_specs=placed,
        out_specs=(P(None, ("dp", "tensor")), *[P("dp", "tensor")] * 6),
        check_vma=False,
    )
```

```python
import functools

import jax
import jax.numpy as jnp
from jax import lax
from jax.experimental import pallas as pl
from jax.experimental.pallas import tpu as pltpu
from jax.sharding import PartitionSpec as P

adapter_scale = 2.0
bias_one = 1.0 - 0.9**10
bias_two = 1.0 - 0.999**10

F32 = jnp.float32
BF16 = jnp.bfloat16
LANES = 128
MIB = 1 << 20


def dot(a, b):
    return jnp.dot(a, b, preferred_element_type=F32)


def dot_nt(a, b):
    length = a.shape[1]
    cut = length // 512 * 256
    if cut < 512:
        return dot_nt_part(a, b, 0, length)
    return dot_nt_part(a, b, 0, cut) + dot_nt_part(a, b, cut, length)


def dot_nt_part(a, b, first, last):
    dims = (((1,), (1,)), ((), ()))
    return lax.dot_general(a[:, first:last], b[:, first:last], dims, preferred_element_type=F32)


def adaptive_moment_step(param, grad, first, second):
    first = 0.9 * first + 0.1 * grad
    second = 0.999 * second + 0.001 * grad * grad
    param = param - 0.004 * (first / bias_one) / (jnp.sqrt(second / bias_two) + 1e-08)
    return (param, first, second)


def tile_of(length, limit):
    units = length // LANES
    return LANES * max(u for u in range(1, limit // LANES + 1) if units % u == 0)


def split_bf16(value):
    high = value.astype(BF16)
    return high, (value - high.astype(F32)).astype(BF16)


def pick(index, choices):
    result = choices[0]
    for at in range(1, len(choices)):
        result = jnp.where(index == at, choices[at], result)
    return result


def shape(dims, kind):
    return jax.ShapeDtypeStruct(dims, kind)


ANY = pl.BlockSpec(memory_space=pl.ANY)
HBM = pl.BlockSpec(memory_space=pltpu.HBM)
VMEM = pl.BlockSpec(memory_space=pltpu.VMEM)


def call(kernel, name, held, far, outputs, far_outputs, scratch, flops, vmem, after=()):
    first = len(held) + len(far)
    moved = sum(a.size * a.dtype.itemsize for a in [*far, *far_outputs])

    def body(*refs):
        kernel(*refs[:first], *refs[first + len(after) :])

    return pl.pallas_call(
        body,
        name=name,
        out_shape=[*outputs, *far_outputs],
        in_specs=[VMEM] * len(held) + [HBM] * len(far) + [ANY] * len(after),
        out_specs=[VMEM] * len(outputs) + [HBM] * len(far_outputs),
        scratch_shapes=scratch,
        compiler_params=pltpu.CompilerParams(vmem_limit_bytes=int(vmem * MIB)),
        cost_estimate=pl.CostEstimate(flops=flops, bytes_accessed=moved, transcendentals=0),
    )(*held, *far, *after)


def in_turn(fetches, ahead=2):
    for fetch in fetches[:ahead]:
        fetch.start()
    done = []

    def arrive():
        fetches[len(done)].wait()
        done.append(True)
        if len(done) - 1 + ahead < len(fetches):
            fetches[len(done) - 1 + ahead].start()

    return arrive


def project_kernel(index, mask, order, far_hidden, far_a, far_cot, far_b, packed, stats, *rest):
    hidden, a, cot, b, arrived = rest
    rank = a.shape[0]
    inner = hidden.shape[1]
    chunks = arrived.shape[0] - 3
    width = inner // chunks
    pairs = [(far_a, a)]
    for at in range(chunks):
        columns = slice(at * width, (at + 1) * width)
        pairs.append((far_hidden.at[:, columns], hidden.at[:, columns]))
    pairs += [(far_cot, cot), (far_b, b)]
    fetches = [pltpu.make_async_copy(*pair, arrived.at[at]) for at, pair in enumerate(pairs)]
    arrive = in_turn(fetches, 3)
    arrive()
    left = a[...].astype(BF16)
    total = None
    for at in range(chunks):
        arrive()
        columns = slice(at * width, (at + 1) * width)
        product = dot_nt(hidden.at[:, columns], left[:, columns])
        total = product if total is None else total + product
    arrive()
    arrive()
    high, low = split_bf16(b[...])
    both = dot_nt(cot, jnp.concatenate([high, low], axis=0))
    both = jnp.concatenate([total, both[:, :rank] + both[:, rank:]], axis=1)
    half = both.shape[0] // 2
    packed[...] = jnp.concatenate([both[:half], both[half:]], axis=1)
    groups, tokens = stats.shape[1], index.shape[1]
    member = (lax.broadcasted_iota(jnp.int32, (groups, tokens), 0) == index[...]).astype(F32)
    row = lax.broadcasted_iota(jnp.int32, (8, tokens), 0)
    values = jnp.where(row == 0, mask[...], 0)
    values = jnp.where(row == 1, mask[...] * order[...], values)
    values = jnp.where(row == 2, mask[...] * order[...] * order[...], values)
    stats[...] = dot_nt(values.astype(F32).astype(BF16), member.astype(BF16))


def gradient_kernel(replicas, rank, all_index, all_mask, all_order, packed, arrived, hidden, cot, *rest):
    stats, (own_a, own_b, *sent) = rest[:replicas], rest[replicas:-2]
    column, grad = rest[-2:]
    rows = rank // replicas
    me = lax.axis_index("dp")
    tokens, inner = hidden.shape
    groups = stats[0].shape[1]
    half = inner // 2
    sums = stats[0][...]
    for other in stats[1:]:
        sums = sums + other[...]
    counts, firsts, squares = sums[0:1, :], sums[1:2, :], sums[2:3, :]
    safe = jnp.maximum(counts, 1.0)
    mean = firsts / safe
    spread = jnp.maximum(jnp.sqrt(jnp.maximum(squares / safe - mean * mean, 0.0)), 1.0)
    total = jnp.maximum(jnp.sum(counts, axis=1, keepdims=True), 1.0)

    row = lax.broadcasted_iota(jnp.int32, (LANES, tokens), 0)
    tall = jnp.where(row == 0, all_index[...], 0)
    tall = jnp.where(row == 1, all_mask[...], tall)
    tall = jnp.where(row == 2, all_order[...], tall)
    column[...] = jnp.transpose(tall.astype(F32))
    index, mask, order = column[:, 0:1], column[:, 1:2], column[:, 2:3]
    member = index == lax.broadcasted_iota(jnp.int32, (tokens, groups), 1).astype(F32)
    own_mean = jnp.sum(jnp.where(member, mean, 0.0), axis=1, keepdims=True)
    own_spread = jnp.sum(jnp.where(member, spread, 0.0), axis=1, keepdims=True)
    coefficient = -mask * (order - own_mean) / own_spread / total

    both = packed[...] + arrived[...]
    both = jnp.concatenate([both[:, : 2 * rank], both[:, 2 * rank : 4 * rank]], axis=0)
    both = both * coefficient
    back = both[:, rank:].astype(BF16).astype(F32)
    high, low = split_bf16(both[:, :rank])
    empty = jnp.zeros((tokens, LANES - 3 * rank), F32)
    tall = jnp.concatenate([back, high.astype(F32), low.astype(F32), empty], axis=1)
    wide = jnp.transpose(tall).astype(BF16)
    grad[...] = adapter_scale * dot(wide[0:rank, :], hidden[...])
    both = dot(wide[rank : 3 * rank, :], cot[...])
    whole = adapter_scale * (both[:rank] + both[rank:])
    pieces = [grad[j * rows : (j + 1) * rows, :] for j in range(replicas)]
    own_a[...] = pick(me, pieces)
    own_b[...] = whole
    folded = [whole[at : at + 2 * rows] for at in range(0, rank, 2 * rows)]
    folded = jnp.concatenate(folded, axis=1).astype(BF16)
    for k in range(1, replicas):
        piece = pick(lax.bitwise_xor(me, k), pieces)
        halves = jnp.concatenate([piece[:, :half], piece[:, half:]], axis=0)
        sent[k - 1][:, 0:half] = halves.astype(BF16)
        sent[k - 1][:, half:] = folded


def update_kernel(replicas, own_a, own_b, x, *rest):
    received, rest = rest[: replicas - 1], rest[replicas - 1 :]
    factors, (sent, out), results = rest[:6], rest[6:8], rest[8:14]
    (a, am, av, b, bm, bv), made, arrived, left = rest[14:20], rest[20:26], rest[26], rest[27]
    rows, inner = a.shape
    rank, columns = b.shape
    me = lax.axis_index("dp")

    def fetch(at):
        source = factors[at]
        if at < 3 and source.shape[0] != rows:
            source = source.at[pl.ds(pl.multiple_of(me * rows, rows), rows), :]
        return pltpu.make_async_copy(source, (a, am, av, b, bm, bv)[at], arrived.at[at])

    def keep(at):
        return pltpu.make_async_copy(made[at], results[at], arrived.at[at])

    for at in range(6):
        fetch(at).start()
    grad_a, grad_b = own_a[...], own_b[...]
    half = inner // 2
    for other in received:
        folded = other[...].astype(F32)
        grad_a = grad_a + jnp.concatenate([folded[:rows, :half], folded[rows:, :half]], axis=1)
        parts = [folded[:, at : at + columns] for at in range(half, folded.shape[1], columns)]
        grad_b = grad_b + jnp.concatenate(parts, axis=0)
    for at in range(6):
        fetch(at).wait()
    made[0][...], made[1][...], made[2][...] = adaptive_moment_step(a[...], grad_a, am[...], av[...])
    padding = jnp.zeros((left.shape[0] - rows, inner), F32)
    left[...] = jnp.concatenate([made[0][...], padding], axis=0).astype(BF16)
    next_b, first_b, second_b = adaptive_moment_step(b[...], grad_b, bm[...], bv[...])
    for array, result in zip((next_b, first_b, second_b), made[3:]):
        result[...] = pick(me, [array[j * rows : (j + 1) * rows] for j in range(replicas)])
    for at in range(6):
        keep(at).start()
    width = columns // replicas
    choices = [next_b[:, j * width : (j + 1) * width] for j in range(replicas)]
    sent[...] = pick(me, choices).astype(BF16)
    product = dot_nt(x, left)
    empty = jnp.zeros((product.shape[0], LANES - left.shape[0]), F32)
    out[...] = jnp.transpose(jnp.concatenate([product, empty], axis=1))[0:rows, :]
    for at in range(6):
        keep(at).wait()


def rollout_kernel(differs, following, first, x, *rest):
    if following is None:
        given, out = rest
    elif first:
        w, out, after, given, arrived = rest
    else:
        given, w, out, after, arrived = rest
    me = lax.axis_index("tensor")
    width = out.shape[1]

    def fetch(differs, held, at):
        start = pl.multiple_of(lax.bitwise_xor(me, differs) * width, width)
        return pltpu.make_async_copy(w.at[:, pl.ds(start, width)], held, arrived.at[at])

    if first:
        own = fetch(differs, given, 0)
        own.start()
        own.wait()
    if following is not None:
        fetch(following, after, 1).start()

    @pl.when(me >= 0)
    def _():
        out[...] = dot(x[...], given[...]).astype(out.dtype)

    if following is not None:
        fetch(following, after, 1).wait()


def gather_kernel(bit, mine, arrived, out):
    later = lax.bitwise_and(lax.shift_right_logical(lax.axis_index("dp"), bit), 1) == 1
    first = jnp.where(later, arrived[...], mine[...])
    out[...] = jnp.concatenate([first, jnp.where(later, mine[...], arrived[...])], axis=0)


def join_kernel(*refs):
    total = refs[0][...].astype(F32)
    for leaf in refs[1:-1]:
        total = total + leaf[...].astype(F32)
    refs[-1][...] = total.astype(refs[-1].dtype)


def finish_kernel(rank, factor, mine, arrived, *rest):
    leaves, (out, made, kept) = rest[:-3], rest[-3:]
    high, low = split_bf16(mine[...] + arrived[...])
    empty = jnp.zeros((LANES - 2 * rank, high.shape[1]), F32)
    wide = jnp.concatenate([high.astype(F32), low.astype(F32), empty], axis=0)
    tall = jnp.transpose(wide).astype(BF16)
    empty = jnp.zeros((LANES - 2 * rank, factor.shape[1]), BF16)
    total = adapter_scale * dot(tall, jnp.concatenate([factor[...], factor[...], empty], axis=0))
    for leaf in leaves:
        total = total + leaf[...].astype(F32)
    made[...] = total.astype(BF16)
    copy = pltpu.make_async_copy(made, out, kept)
    copy.start()
    copy.wait()


def shards(
    hidden,
    cotangent,
    prompt_group_index,
    answer_token_mask,
    token_reward_order,
    source_lowdim_matrix,
    running_mean_source_matrix,
    running_variance_source_matrix,
    target_lowdim_matrix,
    running_mean_target_matrix,
    running_variance_target_matrix,
    frozen_down_weight,
    sampled_token_input,
):
    replicas, peers = lax.axis_size("dp"), lax.axis_size("tensor")
    me_dp = lax.axis_index("dp")
    x, w = sampled_token_input, frozen_down_weight
    tokens, inner = hidden.shape
    columns = cotangent.shape[1]
    rank = source_lowdim_matrix.shape[0]
    rows = rank // replicas
    groups = tokens * replicas // 8
    rollout = x.shape[0]
    own_width = w.shape[1] // peers
    deep = tile_of(inner, 1664)

    def xor(array, k, axis="tensor"):
        return lax.ppermute(array, axis, [(i, i ^ k) for i in range(lax.axis_size(axis))])

    def add(arrays, after=()):
        (total,) = call(
            join_kernel, "join", arrays, [], [shape(arrays[0].shape, arrays[-1].dtype)], [], [], 0, 8, after
        )
        return total

    chips = peers // 2
    todo = [(m, other) for m in range(chips - 1, -1, -1) for other in (1, 0)]
    crossed, arrived, own, waiting, handed = {}, {}, {}, [], None

    def form(eighths, after):
        nonlocal handed
        for _ in range(eighths * len(todo_all) // 8):
            m, other = todo.pop(0)
            following = 2 * todo[0][0] + todo[0][1] if todo else None
            first = handed is None
            outputs = [shape((rollout, own_width), BF16 if other else F32)]
            block = shape((inner, own_width), BF16)
            result, *handed = call(
                functools.partial(rollout_kernel, 2 * m + other, following, first),
                "rollout%d%d" % (m, other),
                [x] if first else [x, handed],
                [] if following is None else [w],
                outputs + ([] if following is None else [block]),
                [],
                ([pltpu.VMEM(block.shape, BF16)] if first else [])
                + ([] if following is None else [pltpu.SemaphoreType.DMA((2,))]),
                2 * rollout * inner * own_width,
                12,
                after,
            )
            handed = handed[0] if handed else None
            if other:
                crossed[m] = xor(result, 1)
            else:
                own[m] = result
                waiting.append(m)
            after = [result]
        return after

    def leaves_of(m):
        bits = [1 << at for at in range(chips.bit_length() - 1)]
        lower = [bit for bit in bits if not m or bit < m & -m]
        return [own[m], crossed[m], *[arrived[m | bit] for bit in lower]]

    def send_on(after):
        while waiting:
            m = waiting.pop(0)
            total = add(leaves_of(m), after)
            arrived[m] = xor(total, 2 * (m & -m))
            after = [total]
        return after

    todo_all = list(todo)

    tok = [
        array.reshape(1, tokens) for array in (prompt_group_index, answer_token_mask, token_reward_order)
    ]
    packed, stats = call(
        project_kernel,
        "project",
        tok,
        [hidden, source_lowdim_matrix, cotangent, target_lowdim_matrix],
        [shape((tokens // 2, LANES), F32), shape((8, groups), F32)],
        [],
        [
            pltpu.VMEM((tokens, inner), BF16),
            pltpu.VMEM((rank, inner), F32),
            pltpu.VMEM((tokens, columns), BF16),
            pltpu.VMEM((rank, columns), F32),
            pltpu.SemaphoreType.DMA((inner // deep + 3,)),
        ],
        2 * tokens * (inner + columns) * 256,
        54,
    )
    all_stats = [stats] + [xor(stats, k, "dp") for k in range(1, replicas)]
    tensor_bits = [1 << at for at in range(peers.bit_length() - 1)]
    received = xor(packed, tensor_bits[0])
    after = form(1, [packed])
    for bit in tensor_bits[1:]:
        packed = add([packed, received], after)
        received = xor(packed, bit)
        after = form(1, [packed]) if bit in (2, 4) else [packed]
    after = send_on(after)

    own_a, own_b, *sent = call(
        functools.partial(gradient_kernel, replicas, rank),
        "gradient",
        [*tok, packed, received, hidden, cotangent, *all_stats],
        [],
        [shape((rows, inner), F32), shape((rank, columns), F32)]
        + [shape((2 * rows, inner // 2 + columns * replicas // 2), BF16)] * (replicas - 1),
        [],
        [pltpu.VMEM((tokens, LANES), F32), pltpu.VMEM((rank, inner), F32)],
        2 * tokens * (inner + columns) * 256,
        16,
        after,
    )
    received = [xor(array, k + 1, "dp") for k, array in enumerate(sent)]
    after = send_on(form(1, [own_a]))

    left = [source_lowdim_matrix, running_mean_source_matrix, running_variance_source_matrix]
    right = [target_lowdim_matrix, running_mean_target_matrix, running_variance_target_matrix]
    if rows % 8:
        left = [lax.dynamic_slice_in_dim(array, me_dp * rows, rows, 0) for array in left]
    own_left, own_right = shape((rows, inner), F32), shape((rows, columns), F32)
    sent_b, product, *updated = call(
        functools.partial(update_kernel, replicas),
        "update",
        [own_a, own_b, x, *received],
        [*left, *right],
        [shape((rank, columns // replicas), BF16), shape((rows, rollout), F32)],
        [own_left] * 3 + [own_right] * 3,
        [pltpu.VMEM((rows, inner), F32)] * 3
        + [pltpu.VMEM((rank, columns), F32)] * 3
        + [pltpu.VMEM((rows, inner), F32)] * 3
        + [pltpu.VMEM((rows, columns), F32)] * 3
        + [pltpu.SemaphoreType.DMA((6,)), pltpu.VMEM((16, inner), BF16)],
        2 * rollout * inner * 256,
        24,
        after,
    )
    pairs = [(dp * peers + at, at * replicas + dp) for dp in range(replicas) for at in range(peers)]
    factor = lax.ppermute(sent_b, ("dp", "tensor"), pairs)
    after = [product]
    for at in range(replicas.bit_length() - 1):
        received = xor(product, 1 << at, "dp")
        if at < 2:
            after = form(1, after)
        if at == replicas.bit_length() - 2:
            after = after + [factor]
        both = shape((2 * product.shape[0], rollout), F32)
        (product,) = call(
            functools.partial(gather_kernel, at), "gather", [product, received], [], [both], [], [], 0, 8, after
        )
        after = [product]
    for at, bit in enumerate(tensor_bits):
        received = xor(product, bit)
        if at < 2 and todo:
            after = form(1 if at == 0 else len(todo) * 8 // len(todo_all), after)
        if at < len(tensor_bits) - 1:
            product = add([product, received], after)
            after = [product]
        if at == 1:
            waiting.remove(0)
            send_on(after)

    (result,) = call(
        functools.partial(finish_kernel, rank),
        "finish",
        [factor, product, received, *leaves_of(0)],
        [],
        [],
        [shape((rollout, own_width), BF16)],
        [pltpu.VMEM((rollout, own_width), BF16), pltpu.SemaphoreType.DMA(())],
        2 * rollout * own_width * 256,
        16,
    )
    return (result, *updated)


def solution(mesh):
    placed = (
        P("dp", "tensor"),
        P("dp", "tensor"),
        P("dp"),
        P("dp"),
        P("dp"),
        P(None, "tensor"),
        P(None, "tensor"),
        P(None, "tensor"),
        P(None, "tensor"),
        P(None, "tensor"),
        P(None, "tensor"),
        P("tensor", "dp"),
        P(None, "tensor"),
    )
    return jax.shard_map(
        shards,
        mesh=mesh,
        in_specs=placed,
        out_specs=(P(None, ("dp", "tensor")), *[P("dp", "tensor")] * 6),
        check_vma=False,
    )
```
